256 devices in a mesh: tm: 64 (over y, z_hi, x), chan: 4 (over z_lo, core).
Axes of the slice: x: 4, y: 4, z: 8 (z_hi: 4, z_lo: 2; z = z_hi * 2 + z_lo), core: 2. Of those that a mesh axis runs over, the one named last changes fastest.
Arguments:
- latents: bfloat16 [512, 256, 512], P('chan', 'tm'), may hold values from -6 to 6
- conv_weight: bfloat16 [512, 3, 9, 512], P(None, None, None, 'chan'), may hold values from -0.0546875 to 0.0546875
- norm_gain: float32 [512], P('chan'), may hold values from 0.1 to 1.9
- norm_bias: float32 [512], P('chan'), may hold values from -3 to 3
- clip_lengths: int32 [12], replicated, may hold values from 1 to 64, 256 in all
- slab_bounds: int32 [64, 2], P('tm'), may hold values from 0 to 256, as said below
Outputs:
- decoded: bfloat16 [512, 512, 512], P('chan', 'tm')
The draws below stay inside these ranges and needn't reach their ends.
Inputs may be any that keep to these rules, and one draw needn't show every extreme that they name: `clip_lengths`: the clips lie end to end and cover all 256 frames; the longest clip has exactly a quarter of 256 frames. `slab_bounds`: slab 0 starts at frame 0, the last slab ends at 256, each slab ends where the next starts, slab s starts within 2 frames of s * 4, so a slab holds 0 to 8 frames; some slab holds exactly 8 frames.
All inputs are finite; a program needn't handle non-finite values.
Results may differ from the reference program's by a relative error of at most 0.001.
Values may be sent and summed in bfloat16 or wider, within the bound.
A program may use at most 128 MiB of HBM per device.

```python
import math
import jax
import jax.numpy as jnp
import numpy as np
from jax import lax

C = 512
GROUPS = 32
FR_DEV = 4
H = 16
W = 32
NCLIP = 12
FRAMES = 256
CAP = 8
N_TM = 64


def draw_slab_bounds(key, part):
    key = jax.random.fold_in(key, 7)
    half_slab = FR_DEV // 2
    shifts = jax.random.randint(key, (N_TM + 1,), -half_slab, half_slab + 1)
    picked = jax.random.randint(jax.random.fold_in(key, 1), (), 1, N_TM - 2)
    position = jnp.arange(N_TM + 1)
    shifts = jnp.where(position == picked, -half_slab, shifts)
    shifts = jnp.where(position == picked + 1, half_slab, shifts)
    shifts = jnp.where((position == 0) | (position == N_TM), 0, shifts)
    starts = position * FR_DEV + shifts
    return jnp.stack([starts[:-1], starts[1:]], axis=1).astype(jnp.int32)


def block_levels(rng, dims, cuts, least, top_value):
    loudness, own = 1.0, jax.random.fold_in(rng, 6)
    for axis_at, blocks in cuts:
        heights = jnp.exp(jax.random.uniform(jax.random.fold_in(own, axis_at), (blocks,), jnp.float32, least / len(cuts), top_value / len(cuts)))
        loudness = loudness * jnp.repeat(heights, dims[axis_at] // blocks).reshape([-1 if axis == axis_at else 1 for axis in range(len(dims))])
    return loudness


def split_up(amount, total, reach, lean):
    weights = [(1 << 20) // math.isqrt(grade ** lean) + 1 for grade in range(2, amount + 1)]
    spare, holding = total - reach - (amount - 1), [1] * (amount - 1)
    while spare > 0:
        candidates = [i for i in range(amount - 1) if holding[i] < reach]
        pool, budget = sum([weights[i] for i in candidates]), spare
        for i in candidates:
            more = min(reach - holding[i], max(1, budget * weights[i] // pool), spare)
            holding[i] = holding[i] + more
            spare = spare - more
    return np.array([reach] + holding)


def uneven_parts(own_key, amount, total, most, skew):
    if amount == 2:
        one = jax.random.randint(own_key, (), max(1, total - most), min(most, total - 1) + 1)
        return jnp.stack([one, total - one])
    tallies = jnp.asarray(split_up(amount, total, most, skew), jnp.int32)
    pairs = (amount - 1) // 2
    giver, sink = tallies[1:1 + 2 * pairs:2], tallies[2:2 + 2 * pairs:2]
    margin = jnp.minimum(giver - 1, most - sink)
    moved = jax.random.randint(jax.random.fold_in(own_key, 1), (pairs,), 0, 1 << 20) % (margin + 1)
    tallies = tallies.at[1:1 + 2 * pairs:2].set(giver - moved).at[2:2 + 2 * pairs:2].set(sink + moved)
    return tallies[jax.random.permutation(jax.random.fold_in(own_key, 2), amount)]


def bell_draw(key, extent, scale, reach, split=(), dtype=jnp.bfloat16):
    level = block_levels(key, extent, split, -0.22, 0.18) if split else 1.0
    entries = jax.random.normal(key, extent, jnp.float32) * scale * level
    return jnp.minimum(jnp.maximum(entries, -reach), reach).astype(dtype)


def setup_inputs(seed: int = 0) -> dict:
    splits = jax.random.split(jax.random.key(seed), 7)
    return {
        "latents": bell_draw(splits[0], (C, FRAMES, H * W), 1.0, 6.0, ((0, 4), (1, 64))),
        "conv_weight": bell_draw(splits[1], (C, 3, 9, C), (27 * C) ** -0.5, 0.0546875, ((3, 4),)),
        "norm_gain": jnp.clip(1.0 + 0.18 * jax.random.normal(splits[2], (C,), jnp.float32), 0.1, 1.9),
        "norm_bias": bell_draw(splits[3], (C,), 0.5, 3.0, ((0, 4),), jnp.float32),
        "clip_lengths": uneven_parts(splits[4], NCLIP, FRAMES, FRAMES // 4, 2).astype(jnp.int32),
        "slab_bounds": draw_slab_bounds(jax.random.fold_in(splits[6], 71), 0),
    }


norm_eps = 1e-06

def frame_starts(clip_lengths, frames):
    clip_ends = jnp.cumsum(clip_lengths)
    starts = clip_ends - clip_lengths
    chosen = jnp.where(starts[None, :] <= frames[:, None], starts[None, :], 0)
    return lax.optimization_barrier(jnp.max(chosen, axis=1)).astype(jnp.int32)

def tap_sources(frames, clip_lengths):
    clip_first = frame_starts(clip_lengths, frames)
    return jnp.stack([jnp.maximum(frames - 2 + offset, clip_first) for offset in range(3)]).astype(jnp.int32)

def columns(extended, local_index):
    channels = extended.shape[0]
    frame_count = local_index.shape[0]
    picked = jnp.take(extended, local_index.astype(jnp.int32), axis=1).reshape(channels, frame_count, H, W)
    padded = jnp.pad(picked, ((0, 0), (0, 0), (1, 1), (1, 1)))
    pieces = [padded[:, :, row_tap:row_tap + H, col_tap:col_tap + W] for row_tap in range(3) for col_tap in range(3)]
    return jnp.stack(pieces).reshape(9 * channels, frame_count * H * W)

def norm_block(summed, residual, norm_gain, norm_bias):
    channels, frame_count, cell_count = summed.shape
    group_width = C // GROUPS
    grouped = summed.reshape(channels // group_width, group_width, frame_count, cell_count)
    average = lax.optimization_barrier(jnp.mean(grouped, axis=(1, 3), keepdims=True))
    variance = lax.optimization_barrier(jnp.mean(jnp.square(grouped - average), axis=(1, 3), keepdims=True))
    normed = ((grouped - average) * lax.rsqrt(variance + norm_eps)).reshape(channels, frame_count, cell_count)
    normed = normed * norm_gain[:, None, None] + norm_bias[:, None, None]
    return (jax.nn.silu(normed) + residual.astype(jnp.float32)).astype(jnp.bfloat16)

def reference(latents, conv_weight, norm_gain, norm_bias, clip_lengths, slab_bounds):
    channels = latents.shape[0]
    weights = [conv_weight[:, offset].reshape(channels, 9 * channels) for offset in range(3)]

    def one_block(block_index):
        frames = (block_index * FR_DEV + jnp.arange(FR_DEV)).astype(jnp.int32)
        sources = tap_sources(frames, clip_lengths)
        summed = jnp.zeros((channels, FR_DEV * H * W), jnp.float32)
        for offset in range(3):
            summed = summed + jnp.dot(weights[offset], columns(latents, sources[offset]), preferred_element_type=jnp.float32)
        residual = jnp.take(latents, frames, axis=1)
        return norm_block(summed.reshape(channels, FR_DEV, H * W), residual, norm_gain, norm_bias)
    blocks = lax.map(one_block, jnp.arange(N_TM).astype(jnp.int32))
    decoded_full = jnp.transpose(blocks, (1, 0, 2, 3)).reshape(channels, FRAMES, H * W)
    slot_index = jnp.arange(CAP).astype(jnp.int32)
    slab_first = slab_bounds[:, 0]
    slab_sizes = slab_bounds[:, 1] - slab_first
    occupied = slot_index[None, :] < slab_sizes[:, None]
    wanted = jnp.where(occupied, slab_first[:, None] + slot_index[None, :], slab_first[:, None]).astype(jnp.int32)
    picked = jnp.take(decoded_full, wanted.reshape(-1), axis=1)
    return jnp.where(occupied.reshape(-1)[None, :, None], picked, jnp.zeros_like(picked))
```

```python
import jax
import jax.numpy as jnp
from jax import lax
from jax.experimental import pallas as pl
from jax.experimental.pallas import tpu as pltpu
from jax.sharding import PartitionSpec as P

MESH = pl.DeviceIdType.MESH
F32 = jnp.float32
BF16 = jnp.bfloat16

GROUPS = 32
NCLIP = 12
FRAMES = 4
CAP = 8
CELLS = 512
ROW = 32
OWN = 128
PAIR = 256
TAPS = 27

N_Y = 3
N_X = 2
Y0 = 0
X0 = Y0 + 4 * N_Y
D0 = X0 + 4 * N_X
N_ZIN = 3
N_ZOUT = TAPS - D0 - N_ZIN
norm_eps = 1e-06


def tap_at(pos):
    return lax.rem(pos, 3) * 9 + lax.div(pos, 3)


def conv_part(w_ref, frames):
    lane = lax.broadcasted_iota(jnp.int32, (1, CELLS), 1)
    column = lax.rem(lane, ROW)
    total = None
    for a in range(3):
        rows = None
        for b in range(3):
            part = None
            for k in range(3):
                term = jnp.dot(w_ref[9 * k + 3 * a + b], frames[k], preferred_element_type=F32)
                part = term if part is None else part + term
            if b == 0:
                part = jnp.where(column > 0, pltpu.roll(part, 1, axis=1), 0.0)
            if b == 2:
                part = jnp.where(column < ROW - 1, pltpu.roll(part, CELLS - 1, axis=1), 0.0)
            rows = part if rows is None else rows + part
        if a == 0:
            rows = jnp.where(lane >= ROW, pltpu.roll(rows, ROW, axis=1), 0.0)
        if a == 2:
            rows = jnp.where(lane < CELLS - ROW, pltpu.roll(rows, CELLS - ROW, axis=1), 0.0)
        total = rows if total is None else total + rows
    return total


def norm_block(summed, residual, gain, bias):
    width = 512 // GROUPS
    grouped = summed.reshape(OWN // width, width, CELLS)
    scale = 1.0 / (width * CELLS)
    average = jnp.sum(jnp.sum(grouped, axis=1, keepdims=True), axis=2, keepdims=True) * scale
    centred = grouped - average
    variance = jnp.sum(jnp.sum(centred * centred, axis=1, keepdims=True), axis=2, keepdims=True) * scale
    normed = (centred * lax.rsqrt(variance + norm_eps)).reshape(OWN, CELLS) * gain + bias
    return (normed / (1.0 + jnp.exp(-normed)) + residual.astype(F32)).astype(BF16)


def kernel(
    clips, bounds, x_ref, w_ref, gain_ref, bias_ref, out_ref,
    xn, xf, wn, wf, acc, blocks, column_pair,
    local_sem, sib_s, sib_r, zx_s, zx_r, fwd_s, fwd_r, halo_s, halo_r, hfwd_s, hfwd_r,
    zw_s, zw_r, xw_s, xw_r, yw_s, yw_r, blk_s, blk_r,
):
    t, c = lax.axis_index("tm"), lax.axis_index("chan")
    p, core = lax.div(c, 2), lax.rem(c, 2)
    y, zh, x = lax.div(t, 16), lax.rem(lax.div(t, 4), 4), lax.rem(t, 4)
    core_else, p_else = 1 - core, 1 - p
    c_sib, c_far, c_cross = 2 * p + core_else, 2 * p_else + core, 2 * p_else + core_else
    zh_out = lax.rem(zh + 3 + 2 * p, 4)
    t_out = (y * 4 + zh_out) * 4 + x

    def along_x(step):
        return (y * 4 + zh) * 4 + lax.rem(x + step, 4)

    def along_y(step):
        return (lax.rem(y + step, 4) * 4 + zh) * 4 + x

    t_next, t_prev = lax.rem(t + 1, 64), lax.rem(t + 63, 64)
    mine = pl.ds(pl.multiple_of(core * OWN, OWN), OWN)
    theirs = pl.ds(pl.multiple_of(core_else * OWN, OWN), OWN)

    barrier = pltpu.get_barrier_semaphore()
    partners = [(t, c_sib), (t, c_far), (t, c_cross), (t_out, c_far), (t_out, c_cross), (t_next, c), (t_prev, c)]
    partners += [(along_x(s), c) for s in (1, 2, 3)] + [(along_y(s), c) for s in (1, 2, 3)]
    for partner in partners:
        pl.semaphore_signal(barrier, inc=1, device_id=partner, device_id_type=MESH)

    def outputs_of(member):
        return pl.ds(pl.multiple_of(member * OWN, OWN), OWN)

    own_w = pltpu.make_async_copy(w_ref.at[:, outputs_of(c), :], wn.at[:, :, mine], local_sem)
    own_w.start()
    for f in range(FRAMES):
        xn[2 + f, mine, :] = x_ref[:, f, :]
    column_pair[0] = jnp.transpose(jnp.broadcast_to(gain_ref[...], (OWN, OWN)))
    column_pair[1] = jnp.transpose(jnp.broadcast_to(bias_ref[...], (OWN, OWN)))
    pl.semaphore_wait(barrier, len(partners))

    def send(src, dst, s, r, device):
        return pltpu.make_async_remote_copy(
            src_ref=src, dst_ref=dst, send_sem=s, recv_sem=r, device_id=device, device_id_type=MESH
        )

    started = []

    def go(copy):
        copy.start()
        started.append(copy)

    order = (2, 3, 0, 1)
    cross = {f: send(xn.at[2 + f, mine], xf.at[2 + f, mine], zx_s.at[f], zx_r.at[f], (t, c_far)) for f in order}
    for f in order:
        go(cross[f])
    sib_x = send(xn.at[pl.ds(2, FRAMES), mine], xn.at[pl.ds(2, FRAMES), mine], sib_s.at[0], sib_r.at[0], (t, c_sib))
    sib_w = send(w_ref.at[:, outputs_of(c_sib), :], wn.at[:, :, mine], sib_s.at[1], sib_r.at[1], (t, c_sib))
    go(sib_x)
    go(sib_w)
    slots = [("y", i) for i in range(N_Y)] + [("x", i) for i in range(N_X)]
    slots += [("d", D0 + i) for i in range(N_ZOUT)] + [("e", D0 + N_ZOUT + i) for i in range(N_ZIN)]

    def place(slot, sx, sy):
        kind, i = slot
        if kind == "y":
            return tap_at(Y0 + N_Y * sy + i)
        if kind == "x":
            return tap_at(X0 + N_X * sx + i)
        return (i % 3) * 9 + i // 3

    fetched = []
    for n, slot in enumerate(slots):
        tap = place(slot, x, y)
        t_to = t if slot[0] == "e" else t_out
        pair = []
        for role, member in enumerate((c_far, c_cross)):
            pair.append(
                send(
                    w_ref.at[tap, outputs_of(member), :], wf.at[tap, :, mine],
                    zw_s.at[n, role], zw_r.at[n, role], (t_to, member),
                )
            )
            go(pair[-1])
        fetched.append(pair)
    for h in range(2):
        go(send(xn.at[4 + h, mine], xn.at[h, mine], halo_s.at[h], halo_r.at[h], (t_next, c)))

    def arrived(src, dst, r):
        pltpu.make_async_remote_copy(
            src_ref=src, dst_ref=dst, send_sem=r, recv_sem=r, device_id=(t, c), device_id_type=MESH
        ).wait_recv()

    def await_weights(n):
        tap = place(slots[n], x, y)
        for role, lanes in enumerate((mine, theirs)):
            arrived(wf.at[tap, :, lanes], wf.at[tap, :, lanes], zw_r.at[n, role])

    def hand_on(n):
        await_weights(n)
        kind, i = slots[n]
        tap = place(slots[n], x, y)
        s, r, to = (yw_s, yw_r, along_y) if kind == "y" else (xw_s, xw_r, along_x)
        for step in (1, 2, 3):
            go(send(wf.at[tap], wf.at[tap], s.at[i, step - 1], r.at[i, step - 1], (to(step), c)))

    def pass_latents(f):
        arrived(xf.at[2 + f, mine], xf.at[2 + f, mine], zx_r.at[f])
        go(send(xf.at[2 + f, mine], xf.at[2 + f, mine], fwd_s.at[f], fwd_r.at[f], (t, c_sib)))
        if f >= 2:
            go(send(xf.at[2 + f, mine], xf.at[f - 2, mine], halo_s.at[f], halo_r.at[f], (t_next, c)))

    def pass_halo(n):
        buffer = xn if n < 2 else xf
        h = n % 2
        arrived(buffer.at[h, mine], buffer.at[h, mine], halo_r.at[n])
        go(send(buffer.at[h, mine], buffer.at[h, mine], hfwd_s.at[n], hfwd_r.at[n], (t, c_sib)))

    def await_halo(n):
        buffer = xn if n < 2 else xf
        h = n % 2
        arrived(buffer.at[h, theirs], buffer.at[h, theirs], hfwd_r.at[n])

    def sources(buffer, f):
        frame = t * FRAMES + f
        first, end = jnp.int32(0), jnp.int32(0)
        for n in range(NCLIP):
            first = jnp.where(end <= frame, end, first)
            end = end + clips[n]
        own = buffer[f + 2]
        before = jnp.where(first <= frame - 1, buffer[f + 1], own)
        earlier = jnp.where(first <= frame - 2, buffer[f], before)
        return earlier, before, own

    def near(f):
        acc[f] = conv_part(wn, sources(xn, f))

    own_w.wait()
    arrived(xn.at[pl.ds(2, FRAMES), theirs], xn.at[pl.ds(2, FRAMES), theirs], sib_r.at[0])
    arrived(wn.at[:, :, theirs], wn.at[:, :, theirs], sib_r.at[1])

    near(3)
    hand_on(0)
    pass_latents(2)
    near(2)
    hand_on(1)
    pass_halo(0)
    pass_halo(1)
    hand_on(2)
    pass_latents(3)
    await_halo(0)
    await_halo(1)
    near(1)
    hand_on(3)
    hand_on(4)
    near(0)
    pass_latents(0)
    pass_halo(2)
    pass_halo(3)
    pass_latents(1)

    for f in order:
        arrived(xf.at[2 + f, theirs], xf.at[2 + f, theirs], fwd_r.at[f])
    await_halo(2)
    await_halo(3)
    for n in range(N_Y + N_X, len(slots)):
        await_weights(n)
    for kind, count, r in (("x", N_X, xw_r), ("y", N_Y, yw_r)):
        for i in range(count):
            for step in (1, 2, 3):
                tap = place((kind, i), lax.rem(x + 4 - step, 4), lax.rem(y + 4 - step, 4))
                arrived(wf.at[tap], wf.at[tap], r.at[i, step - 1])

    gain, bias = column_pair[0, :, 0:1], column_pair[1, :, 0:1]
    sent = {}
    for f in (1, 2, 0, 3):
        summed = acc[f] + conv_part(wf, sources(xf, f))
        blocks[2 + f] = norm_block(summed, xn[2 + f, mine, :], gain, bias)
        to, slot = (t_prev, 6 + f) if f < 2 else (t_next, f - 2)
        go(send(blocks.at[2 + f], blocks.at[slot], blk_s.at[f], blk_r.at[f], (to, c)))
    for f in range(FRAMES):
        slot = 6 + f if f < 2 else f - 2
        arrived(blocks.at[slot], blocks.at[slot], blk_r.at[f])

    first, size = bounds[0, 0], bounds[0, 1] - bounds[0, 0]
    offset = first - (t * FRAMES - 2)
    columns = []
    for j in range(CAP):
        value = blocks[jnp.clip(offset + j, 0, CAP - 1)]
        columns.append(jnp.where(j < size, value, jnp.zeros_like(value)).astype(F32))
    out_ref[...] = jnp.stack(columns, axis=1).astype(BF16)
    for copy in started:
        copy.wait_send()


def shards(latents, conv_weight, norm_gain, norm_bias, clip_lengths, slab_bounds):
    weights = jnp.transpose(conv_weight, (1, 2, 0, 3)).reshape(TAPS, 512, OWN)
    vmem, smem, dma = pltpu.VMEM, pltpu.SMEM, pltpu.SemaphoreType.DMA
    n_slots = N_Y + N_X + N_ZOUT + N_ZIN
    return pl.pallas_call(
        kernel,
        out_shape=jax.ShapeDtypeStruct((OWN, CAP, CELLS), BF16),
        in_specs=[
            pl.BlockSpec(memory_space=smem),
            pl.BlockSpec(memory_space=smem),
            pl.BlockSpec(memory_space=vmem),
            pl.BlockSpec(memory_space=pl.ANY),
            pl.BlockSpec(memory_space=vmem),
            pl.BlockSpec(memory_space=vmem),
        ],
        out_specs=pl.BlockSpec(memory_space=vmem),
        scratch_shapes=[
            vmem((6, PAIR, CELLS), BF16),
            vmem((6, PAIR, CELLS), BF16),
            vmem((TAPS, OWN, PAIR), BF16),
            vmem((TAPS, OWN, PAIR), BF16),
            vmem((FRAMES, OWN, CELLS), F32),
            vmem((CAP, OWN, CELLS), BF16),
            vmem((2, OWN, OWN), F32),
            dma,
            dma((2,)), dma((2,)),
            dma((4,)), dma((4,)),
            dma((4,)), dma((4,)),
            dma((4,)), dma((4,)),
            dma((4,)), dma((4,)),
            dma((n_slots, 2)), dma((n_slots, 2)),
            dma((N_X, 3)), dma((N_X, 3)),
            dma((N_Y, 3)), dma((N_Y, 3)),
            dma((4,)), dma((4,)),
        ],
        compiler_params=pltpu.CompilerParams(
            collective_id=0, has_side_effects=True, vmem_limit_bytes=56 * 2**20
        ),
    )(clip_lengths, slab_bounds, latents, weights, norm_gain.reshape(1, OWN), norm_bias.reshape(1, OWN))


def solution(mesh):
    placed = (P("chan", "tm", None), P(None, None, None, "chan"), P("chan"), P("chan"), P(), P("tm", None))
    return jax.shard_map(
        shards, mesh=mesh, in_specs=placed, out_specs=P("chan", "tm", None), check_vma=False
    )
```

```python
import jax
import jax.numpy as jnp
from jax import lax
from jax.experimental import pallas as pl
from jax.experimental.pallas import tpu as pltpu
from jax.sharding import PartitionSpec as P

MESH = pl.DeviceIdType.MESH
F32 = jnp.float32
BF16 = jnp.bfloat16

GROUPS = 32
NCLIP = 12
SLABS = 64
FRAMES = 4
CAP = 8
CELLS = 512
ROW = 32
OWN = 128
PAIR = 256
TAPS = 27
WIDTH = 512 // GROUPS
norm_eps = 1e-06


def conv_part(w_ref, side, frames):
    lane = lax.broadcasted_iota(jnp.int32, (1, CELLS), 1)
    column = lax.rem(lane, ROW)
    total = None
    for a in range(3):
        rows = None
        for b in range(3):
            part = None
            for k in range(3):
                tap = 9 * k + 3 * a + b
                weights = jnp.concatenate([w_ref[side, tap, 0], w_ref[side, tap, 1]], axis=1)
                term = jnp.dot(weights, frames[k], preferred_element_type=F32)
                part = term if part is None else part + term
            if b == 0:
                part = jnp.where(column > 0, pltpu.roll(part, 1, axis=1), 0.0)
            if b == 2:
                part = jnp.where(column < ROW - 1, pltpu.roll(part, CELLS - 1, axis=1), 0.0)
            rows = part if rows is None else rows + part
        if a == 0:
            rows = jnp.where(lane >= ROW, pltpu.roll(rows, ROW, axis=1), 0.0)
        if a == 2:
            rows = jnp.where(lane < CELLS - ROW, pltpu.roll(rows, CELLS - ROW, axis=1), 0.0)
        total = rows if total is None else total + rows
    return total


def norm_block(summed, residual, gain, bias):
    grouped = summed.reshape(OWN // WIDTH, WIDTH, CELLS)
    scale = 1.0 / (WIDTH * CELLS)
    average = jnp.sum(jnp.sum(grouped, axis=1, keepdims=True), axis=2, keepdims=True) * scale
    centred = grouped - average
    variance = jnp.sum(jnp.sum(centred * centred, axis=1, keepdims=True), axis=2, keepdims=True) * scale
    normed = (centred * lax.rsqrt(variance + norm_eps)).reshape(OWN, CELLS) * gain + bias
    return (normed / (1.0 + jnp.exp(-normed)) + residual.astype(F32)).astype(BF16)


def coded(summed):
    grouped = summed.reshape(OWN // WIDTH, WIDTH, CELLS)
    top = jnp.max(jnp.max(jnp.abs(grouped), axis=1, keepdims=True), axis=2, keepdims=True)
    step = jnp.maximum(top, 1e-30) * (1.0 / 32767.0)
    levels = jnp.round(grouped * (1.0 / step)).reshape(OWN, CELLS)
    return levels.astype(jnp.int32).astype(jnp.int16), jnp.broadcast_to(step.reshape(OWN // WIDTH, 1), (OWN // WIDTH, OWN))


def decoded(levels, steps):
    grouped = levels.astype(jnp.int32).astype(F32).reshape(OWN // WIDTH, WIDTH, CELLS)
    return (grouped * steps[:, 0:1].reshape(OWN // WIDTH, 1, 1)).reshape(OWN, CELLS)


def kernel(
    clips, bounds, x_ref, w_ref, gain_ref, bias_ref, out_ref,
    xn, weights, acc, q_out, q_in, step_out, step_in, blocks, column_pair,
    local_sem, sib_s, sib_r, halo_s, halo_r, hfwd_s, hfwd_r, q_s, q_r, step_s, step_r, blk_s, blk_r,
):
    t, c = lax.axis_index("tm"), lax.axis_index("chan")
    p, core = lax.div(c, 2), lax.rem(c, 2)
    core_else = 1 - core
    c_sib, c_far, c_cross = 2 * p + core_else, 2 * (1 - p) + core, 2 * (1 - p) + core_else
    t_next, t_prev = lax.rem(t + 1, SLABS), lax.rem(t + SLABS - 1, SLABS)
    has_next, has_prev = t < SLABS - 1, t > 0
    mine = pl.ds(pl.multiple_of(core * OWN, OWN), OWN)
    theirs = pl.ds(pl.multiple_of(core_else * OWN, OWN), OWN)

    barrier = pltpu.get_barrier_semaphore()

    def greet(partner):
        pl.semaphore_signal(barrier, inc=1, device_id=partner, device_id_type=MESH)

    greet((t, c_sib))
    greet((t, c_far))
    pl.when(has_next)(lambda: greet((t_next, c)))
    pl.when(has_prev)(lambda: greet((t_prev, c)))

    def outputs_of(member):
        return pl.ds(pl.multiple_of(member * OWN, OWN), OWN)

    own_w = [
        pltpu.make_async_copy(w_ref.at[:, outputs_of(member), :], weights.at[side, :, core], local_sem.at[side])
        for side, member in enumerate((c_far, c))
    ]
    for copy in own_w:
        copy.start()
    for f in range(FRAMES):
        xn[2 + f, mine, :] = x_ref[:, f, :]
    column_pair[0] = jnp.transpose(jnp.broadcast_to(gain_ref[...], (OWN, OWN)))
    column_pair[1] = jnp.transpose(jnp.broadcast_to(bias_ref[...], (OWN, OWN)))
    pl.semaphore_wait(barrier, 2 + has_next.astype(jnp.int32) + has_prev.astype(jnp.int32))

    def send(src, dst, s, r, device):
        return pltpu.make_async_remote_copy(
            src_ref=src, dst_ref=dst, send_sem=s, recv_sem=r, device_id=device, device_id_type=MESH
        )

    started = []

    def go(copy, when=None):
        if when is None:
            copy.start()
        else:
            pl.when(when)(copy.start)
        started.append((copy, when))

    go(send(xn.at[pl.ds(2, FRAMES), mine], xn.at[pl.ds(2, FRAMES), mine], sib_s.at[2], sib_r.at[2], (t, c_sib)))
    for side, member in enumerate((c_cross, c_sib)):
        go(send(w_ref.at[:, outputs_of(member), :], weights.at[side, :, core], sib_s.at[side], sib_r.at[side], (t, c_sib)))
    for h in (1, 0):
        go(send(xn.at[4 + h, mine], xn.at[h, mine], halo_s.at[h], halo_r.at[h], (t_next, c)), has_next)

    def arrived(dst, r, when=None):
        copy = pltpu.make_async_remote_copy(
            src_ref=dst, dst_ref=dst, send_sem=r, recv_sem=r, device_id=(t, c), device_id_type=MESH
        )
        if when is None:
            copy.wait_recv()
        else:
            pl.when(when)(copy.wait_recv)

    def pass_halo(h):
        arrived(xn.at[h, mine], halo_r.at[h], has_prev)
        go(send(xn.at[h, mine], xn.at[h, mine], hfwd_s.at[h], hfwd_r.at[h], (t, c_sib)), has_prev)

    def sources(f):
        frame = t * FRAMES + f
        first, end = jnp.int32(0), jnp.int32(0)
        for n in range(NCLIP):
            first = jnp.where(end <= frame, end, first)
            end = end + clips[n]
        own = xn[f + 2]
        before = jnp.where(first <= frame - 1, xn[f + 1], own)
        earlier = jnp.where(first <= frame - 2, xn[f], before)
        return earlier, before, own

    def theirs_of(f):
        levels, steps = coded(conv_part(weights, 0, sources(f)))
        q_out[f] = levels
        step_out[f] = steps
        go(send(q_out.at[f], q_in.at[f], q_s.at[f], q_r.at[f], (t, c_far)))
        go(send(step_out.at[f], step_in.at[f], step_s.at[f], step_r.at[f], (t, c_far)))

    def own_of(f):
        acc[f] = conv_part(weights, 1, sources(f))

    def finish(f):
        arrived(q_in.at[f], q_r.at[f])
        arrived(step_in.at[f], step_r.at[f])
        summed = acc[f] + decoded(q_in[f], step_in[f])
        gain, bias = column_pair[0, :, 0:1], column_pair[1, :, 0:1]
        blocks[2 + f] = norm_block(summed, xn[2 + f, mine, :], gain, bias)
        to, slot, when = (t_prev, 6 + f, has_prev) if f < 2 else (t_next, f - 2, has_next)
        go(send(blocks.at[2 + f], blocks.at[slot], blk_s.at[f], blk_r.at[f], (to, c)), when)

    @pl.when(jnp.logical_not(has_prev))
    def _():
        for h in range(2):
            xn[h] = jnp.zeros((PAIR, CELLS), BF16)
            blocks[h] = jnp.zeros((OWN, CELLS), BF16)

    @pl.when(jnp.logical_not(has_next))
    def _():
        for h in range(2):
            blocks[6 + h] = jnp.zeros((OWN, CELLS), BF16)

    own_w[0].wait()
    arrived(xn.at[pl.ds(2, FRAMES), theirs], sib_r.at[2])
    arrived(weights.at[0, :, core_else], sib_r.at[0])
    theirs_of(3)
    theirs_of(2)
    own_w[1].wait()
    arrived(weights.at[1, :, core_else], sib_r.at[1])
    own_of(3)
    pass_halo(1)
    own_of(2)
    pass_halo(0)
    arrived(xn.at[1, theirs], hfwd_r.at[1], has_prev)
    theirs_of(1)
    arrived(xn.at[0, theirs], hfwd_r.at[0], has_prev)
    theirs_of(0)
    finish(3)
    finish(2)
    own_of(1)
    own_of(0)
    finish(1)
    finish(0)

    for f in range(FRAMES):
        slot, when = (6 + f, has_next) if f < 2 else (f - 2, has_prev)
        arrived(blocks.at[slot], blk_r.at[f], when)

    first, size = bounds[0, 0], bounds[0, 1] - bounds[0, 0]
    offset = first - (t * FRAMES - 2)
    columns = []
    for j in range(CAP):
        value = blocks[jnp.clip(offset + j, 0, CAP - 1)]
        columns.append(jnp.where(j < size, value, jnp.zeros_like(value)).astype(F32))
    out_ref[...] = jnp.stack(columns, axis=1).astype(BF16)
    for copy, when in started:
        if when is None:
            copy.wait_send()
        else:
            pl.when(when)(copy.wait_send)


def shards(latents, conv_weight, norm_gain, norm_bias, clip_lengths, slab_bounds):
    weights = jnp.transpose(conv_weight, (1, 2, 0, 3)).reshape(TAPS, 512, OWN)
    vmem, smem, dma = pltpu.VMEM, pltpu.SMEM, pltpu.SemaphoreType.DMA
    return pl.pallas_call(
        kernel,
        out_shape=jax.ShapeDtypeStruct((OWN, CAP, CELLS), BF16),
        in_specs=[
            pl.BlockSpec(memory_space=smem),
            pl.BlockSpec(memory_space=smem),
            pl.BlockSpec(memory_space=vmem),
            pl.BlockSpec(memory_space=pl.ANY),
            pl.BlockSpec(memory_space=vmem),
            pl.BlockSpec(memory_space=vmem),
        ],
        out_specs=pl.BlockSpec(memory_space=vmem),
        scratch_shapes=[
            vmem((6, PAIR, CELLS), BF16),
            vmem((2, TAPS, 2, OWN, OWN), BF16),
            vmem((FRAMES, OWN, CELLS), F32),
            vmem((FRAMES, OWN, CELLS), jnp.int16),
            vmem((FRAMES, OWN, CELLS), jnp.int16),
            vmem((FRAMES, OWN // WIDTH, OWN), F32),
            vmem((FRAMES, OWN // WIDTH, OWN), F32),
            vmem((CAP, OWN, CELLS), BF16),
            vmem((2, OWN, OWN), F32),
            dma((2,)),
            dma((3,)), dma((3,)),
            dma((2,)), dma((2,)),
            dma((2,)), dma((2,)),
            dma((4,)), dma((4,)),
            dma((4,)), dma((4,)),
            dma((4,)), dma((4,)),
        ],
        compiler_params=pltpu.CompilerParams(
            collective_id=0, has_side_effects=True, vmem_limit_bytes=56 * 2**20
        ),
    )(clip_lengths, slab_bounds, latents, weights, norm_gain.reshape(1, OWN), norm_bias.reshape(1, OWN))


def solution(mesh):
    placed = (P("chan", "tm", None), P(None, None, None, "chan"), P("chan"), P("chan"), P(), P("tm", None))
    return jax.shard_map(
        shards, mesh=mesh, in_specs=placed, out_specs=P("chan", "tm", None), check_vma=False
    )
```

```python
import jax
import jax.numpy as jnp
from jax import lax
from jax.experimental import pallas as pl
from jax.experimental.pallas import tpu as pltpu
from jax.sharding import PartitionSpec as P

MESH = pl.DeviceIdType.MESH
F32 = jnp.float32
BF16 = jnp.bfloat16

GROUPS = 32
NCLIP = 12
SLABS = 64
RING = 4
MOST = 6
FRAMES = 4
CAP = 8
CELLS = 512
ROW = 32
OWN = 128
PAIR = 256
TAPS = 27
WIDTH = 512 // GROUPS
norm_eps = 1e-06


def conv_part(w_ref, side, frames):
    lane = lax.broadcasted_iota(jnp.int32, (1, CELLS), 1)
    column = lax.rem(lane, ROW)
    total = None
    for a in range(3):
        rows = None
        for b in range(3):
            part = None
            for k in range(3):
                tap = 9 * k + 3 * a + b
                weights = jnp.concatenate([w_ref[side, tap, 0], w_ref[side, tap, 1]], axis=1)
                term = jnp.dot(weights, frames[k], preferred_element_type=F32)
                part = term if part is None else part + term
            if b == 0:
                part = jnp.where(column > 0, pltpu.roll(part, 1, axis=1), 0.0)
            if b == 2:
                part = jnp.where(column < ROW - 1, pltpu.roll(part, CELLS - 1, axis=1), 0.0)
            rows = part if rows is None else rows + part
        if a == 0:
            rows = jnp.where(lane >= ROW, pltpu.roll(rows, ROW, axis=1), 0.0)
        if a == 2:
            rows = jnp.where(lane < CELLS - ROW, pltpu.roll(rows, CELLS - ROW, axis=1), 0.0)
        total = rows if total is None else total + rows
    return total


def norm_block(summed, residual, gain, bias):
    grouped = summed.reshape(OWN // WIDTH, WIDTH, CELLS)
    scale = 1.0 / (WIDTH * CELLS)
    average = jnp.sum(jnp.sum(grouped, axis=1, keepdims=True), axis=2, keepdims=True) * scale
    centred = grouped - average
    variance = jnp.sum(jnp.sum(centred * centred, axis=1, keepdims=True), axis=2, keepdims=True) * scale
    normed = (centred * lax.rsqrt(variance + norm_eps)).reshape(OWN, CELLS) * gain + bias
    return (normed / (1.0 + jnp.exp(-normed)) + residual.astype(F32)).astype(BF16)


def coded(summed):
    grouped = summed.reshape(OWN // WIDTH, WIDTH, CELLS)
    top = jnp.max(jnp.max(jnp.abs(grouped), axis=1, keepdims=True), axis=2, keepdims=True)
    step = jnp.maximum(top, 1e-30) * (1.0 / 32767.0)
    levels = jnp.round(grouped * (1.0 / step)).reshape(OWN, CELLS)
    return levels.astype(jnp.int32).astype(jnp.int16), jnp.broadcast_to(step.reshape(OWN // WIDTH, 1), (OWN // WIDTH, OWN))


def decoded(levels, steps):
    grouped = levels.astype(jnp.int32).astype(F32).reshape(OWN // WIDTH, WIDTH, CELLS)
    return (grouped * steps[:, 0:1].reshape(OWN // WIDTH, 1, 1)).reshape(OWN, CELLS)


def kernel(
    clips, bounds, x_ref, w_ref, gain_ref, bias_ref, out_ref,
    xn, weights, acc, q_out, q_in, step_out, step_in, blocks, column_pair, relay,
    local_sem, sib_s, sib_r, halo_s, halo_r, hfwd_s, hfwd_r, q_s, q_r, step_s, step_r, blk_s, blk_r, relay_s, relay_r, ext_s, ext_r, efwd_s, efwd_r,
):
    t, c = lax.axis_index("tm"), lax.axis_index("chan")
    p, core = lax.div(c, 2), lax.rem(c, 2)
    core_else = 1 - core
    c_sib, c_far, c_cross = 2 * p + core_else, 2 * (1 - p) + core, 2 * (1 - p) + core_else
    t_next, t_prev = lax.rem(t + 1, SLABS), lax.rem(t + SLABS - 1, SLABS)
    has_next, has_prev = t < SLABS - 1, t > 0
    x = lax.rem(t, RING)
    at_low, at_high = x == 0, x == RING - 1
    not_low, not_high = x > 0, x < RING - 1
    ring_next, ring_prev = t < SLABS - RING, t >= RING

    def slab(step):
        return lax.rem(t + SLABS + step, SLABS)

    extra = at_high & has_next
    mine = pl.ds(pl.multiple_of(core * OWN, OWN), OWN)
    theirs = pl.ds(pl.multiple_of(core_else * OWN, OWN), OWN)

    barrier = pltpu.get_barrier_semaphore()

    def greet(partner):
        pl.semaphore_signal(barrier, inc=1, device_id=partner, device_id_type=MESH)

    partners = [(has_next, 1), (has_prev, -1), (at_high, -2), (at_high, -3)]
    partners += [((x == 2) & ring_next, 2), (x == 1, 2), ((x == 1) & ring_next, 3)]
    partners += [(at_low, 3), (at_low & ring_next, 4)] + [(at_low & ring_prev, -step) for step in (2, 3, 4)]
    greet((t, c_sib))
    greet((t, c_far))
    for when, step in partners:
        pl.when(when)(lambda step=step: greet((slab(step), c)))

    def outputs_of(member):
        return pl.ds(pl.multiple_of(member * OWN, OWN), OWN)

    own_w = [
        pltpu.make_async_copy(w_ref.at[:, outputs_of(member), :], weights.at[side, :, core], local_sem.at[side])
        for side, member in enumerate((c_far, c))
    ]
    for copy in own_w:
        copy.start()
    for f in range(FRAMES):
        xn[2 + f, mine, :] = x_ref[:, f, :]
    column_pair[0] = jnp.transpose(jnp.broadcast_to(gain_ref[...], (OWN, OWN)))
    column_pair[1] = jnp.transpose(jnp.broadcast_to(bias_ref[...], (OWN, OWN)))
    pl.semaphore_wait(barrier, 2 + sum(when.astype(jnp.int32) for when, _ in partners))

    def send(src, dst, s, r, device):
        return pltpu.make_async_remote_copy(
            src_ref=src, dst_ref=dst, send_sem=s, recv_sem=r, device_id=device, device_id_type=MESH
        )

    started = []

    def go(copy, when=None, keep=True):
        if when is None:
            copy.start()
        else:
            pl.when(when)(copy.start)
        if keep:
            started.append((copy, when))

    go(send(xn.at[pl.ds(2, FRAMES), mine], xn.at[pl.ds(2, FRAMES), mine], sib_s.at[2], sib_r.at[2], (t, c_sib)))
    for side, member in enumerate((c_cross, c_sib)):
        go(send(w_ref.at[:, outputs_of(member), :], weights.at[side, :, core], sib_s.at[side], sib_r.at[side], (t, c_sib)))
    go(send(xn.at[5, mine], xn.at[1, mine], halo_s.at[1], halo_r.at[1], (t_next, c)), has_next)
    go(send(xn.at[4, mine], xn.at[0, mine], halo_s.at[0], halo_r.at[0], (t_next, c)), has_next & not_high)
    go(send(xn.at[4, mine], relay.at[0], halo_s.at[0], relay_r.at[0], (slab(-3), c)), has_next & at_high)

    for h in range(2):
        go(send(xn.at[2 + h, mine], xn.at[6 + h, mine], ext_s.at[h], ext_r.at[h], (t_prev, c)), has_prev & at_low)

    def arrived(dst, r, when=None):
        copy = pltpu.make_async_remote_copy(
            src_ref=dst, dst_ref=dst, send_sem=r, recv_sem=r, device_id=(t, c), device_id_type=MESH
        )
        if when is None:
            copy.wait_recv()
        else:
            pl.when(when)(copy.wait_recv)

    passed = [send(xn.at[h, mine], xn.at[h, mine], hfwd_s.at[h], hfwd_r.at[h], (t, c_sib)) for h in range(2)]
    started += [(copy, has_prev) for copy in passed]

    def pass_halo(h):
        arrived(xn.at[h, mine], halo_r.at[h])
        passed[h].start()
        arrived(xn.at[h, theirs], hfwd_r.at[h])

    def relay_on(n, place, dst, r, step):
        when = (x == place) & ring_next
        arrived(relay.at[n], relay_r.at[n], when)
        go(send(relay.at[n], dst, relay_s.at[n], r, (slab(step), c)), when)

    extra_passed = [send(xn.at[6 + h, mine], xn.at[6 + h, mine], efwd_s.at[h], efwd_r.at[h], (t, c_sib)) for h in range(2)]
    started += [(copy, extra) for copy in extra_passed]

    def pass_extra(h):
        arrived(xn.at[6 + h, mine], ext_r.at[h])
        extra_passed[h].start()
        arrived(xn.at[6 + h, theirs], efwd_r.at[h])

    def sources(f):
        frame = t * FRAMES + f
        first, end = jnp.int32(0), jnp.int32(0)
        for n in range(NCLIP):
            first = jnp.where(end <= frame, end, first)
            end = end + clips[n]
        own = xn[f + 2]
        before = jnp.where(first <= frame - 1, xn[f + 1], own)
        earlier = jnp.where(first <= frame - 2, xn[f], before)
        return earlier, before, own

    def theirs_of(f, keep=True):
        levels, steps = coded(conv_part(weights, 0, sources(f)))
        q_out[f] = levels
        step_out[f] = steps
        go(send(q_out.at[f], q_in.at[f], q_s.at[f], q_r.at[f], (t, c_far)), None, keep)
        go(send(step_out.at[f], step_in.at[f], step_s.at[f], step_r.at[f], (t, c_far)), None, keep)

    def own_of(f):
        acc[f] = conv_part(weights, 1, sources(f))

    def merge(f):
        arrived(q_in.at[f], q_r.at[f])
        arrived(step_in.at[f], step_r.at[f])
        summed = acc[f] + decoded(q_in[f], step_in[f])
        gain, bias = column_pair[0, :, 0:1], column_pair[1, :, 0:1]
        blocks[2 + f] = norm_block(summed, xn[2 + f, mine, :], gain, bias)

    def finish(f):
        merge(f)
        if f < 2:
            go(send(blocks.at[2 + f], blocks.at[6 + f], blk_s.at[f], blk_r.at[f], (t_prev, c)), has_prev & not_low)
            return
        go(send(blocks.at[2 + f], blocks.at[f - 2], blk_s.at[f], blk_r.at[f], (t_next, c)), has_next & not_high)
        n, to = (1, slab(-1)) if f == 3 else (2, slab(-2))
        go(send(blocks.at[2 + f], relay.at[n], blk_s.at[f], relay_r.at[n], (to, c)), has_next & at_high)

    @pl.when(jnp.logical_not(has_prev))
    def _():
        for h in range(2):
            xn[h] = jnp.zeros((PAIR, CELLS), BF16)
            blocks[h] = jnp.zeros((OWN, CELLS), BF16)

    @pl.when(jnp.logical_not(has_next))
    def _():
        for h in range(2):
            blocks[6 + h] = jnp.zeros((OWN, CELLS), BF16)

    own_w[0].wait()
    arrived(xn.at[pl.ds(2, FRAMES), theirs], sib_r.at[2])
    arrived(weights.at[0, :, core_else], sib_r.at[0])
    theirs_of(3)
    theirs_of(2)
    own_w[1].wait()
    arrived(weights.at[1, :, core_else], sib_r.at[1])
    own_of(3)
    pl.when(not_low)(lambda: pass_halo(1))
    relay_on(0, 0, xn.at[0, mine], halo_r.at[0], 4)
    own_of(2)
    pl.when(at_low & has_prev)(lambda: pass_halo(1))
    pl.when(not_low)(lambda: pass_halo(0))
    theirs_of(1)
    finish(3)
    pl.when(not_low)(lambda: theirs_of(0, False))
    finish(2)
    own_of(1)
    pl.when(at_low & has_prev)(lambda: pass_halo(0))
    pl.when(at_low)(lambda: theirs_of(0, False))
    own_of(0)
    relay_on(1, 2, blocks.at[1], blk_r.at[3], 2)

    @pl.when(extra)
    def _():
        pass_extra(0)
        pass_extra(1)
        lax.fori_loop(FRAMES, FRAMES + 2, lambda f, carry: (theirs_of(f, False), carry)[1], 0)

    finish(1)
    relay_on(2, 1, blocks.at[0], blk_r.at[2], 3)
    finish(0)

    @pl.when(extra)
    def _():
        def both(f, carry):
            own_of(f)
            merge(f)
            return carry

        lax.fori_loop(FRAMES, FRAMES + 2, both, 0)

    for f in range(FRAMES):
        slot, when = (6 + f, has_next & not_high) if f < 2 else (f - 2, has_prev)
        arrived(blocks.at[slot], blk_r.at[f], when)

    first, size = bounds[0, 0], bounds[0, 1] - bounds[0, 0]
    offset = first - (t * FRAMES - 2)
    columns = []
    for j in range(CAP):
        value = blocks[jnp.clip(offset + j, 0, CAP - 1)]
        columns.append(jnp.where(j < size, value, jnp.zeros_like(value)).astype(F32))
    out_ref[...] = jnp.stack(columns, axis=1).astype(BF16)
    for f, when in ((0, None), (4, extra), (5, extra)):
        started.append((send(q_out.at[f], q_in.at[f], q_s.at[f], q_r.at[f], (t, c_far)), when))
        started.append((send(step_out.at[f], step_in.at[f], step_s.at[f], step_r.at[f], (t, c_far)), when))
    for copy, when in started:
        if when is None:
            copy.wait_send()
        else:
            pl.when(when)(copy.wait_send)


def shards(latents, conv_weight, norm_gain, norm_bias, clip_lengths, slab_bounds):
    weights = jnp.transpose(conv_weight, (1, 2, 0, 3)).reshape(TAPS, 512, OWN)
    vmem, smem, dma = pltpu.VMEM, pltpu.SMEM, pltpu.SemaphoreType.DMA
    return pl.pallas_call(
        kernel,
        out_shape=jax.ShapeDtypeStruct((OWN, CAP, CELLS), BF16),
        in_specs=[
            pl.BlockSpec(memory_space=smem),
            pl.BlockSpec(memory_space=smem),
            pl.BlockSpec(memory_space=vmem),
            pl.BlockSpec(memory_space=pl.ANY),
            pl.BlockSpec(memory_space=vmem),
            pl.BlockSpec(memory_space=vmem),
        ],
        out_specs=pl.BlockSpec(memory_space=vmem),
        scratch_shapes=[
            vmem((CAP, PAIR, CELLS), BF16),
            vmem((2, TAPS, 2, OWN, OWN), BF16),
            vmem((MOST, OWN, CELLS), F32),
            vmem((MOST, OWN, CELLS), jnp.int16),
            vmem((MOST, OWN, CELLS), jnp.int16),
            vmem((MOST, OWN // WIDTH, OWN), F32),
            vmem((MOST, OWN // WIDTH, OWN), F32),
            vmem((CAP, OWN, CELLS), BF16),
            vmem((2, OWN, OWN), F32),
            vmem((3, OWN, CELLS), BF16),
            dma((2,)),
            dma((3,)), dma((3,)),
            dma((2,)), dma((2,)),
            dma((2,)), dma((2,)),
            dma((MOST,)), dma((MOST,)),
            dma((MOST,)), dma((MOST,)),
            dma((4,)), dma((4,)),
            dma((3,)), dma((3,)),
            dma((2,)), dma((2,)),
            dma((2,)), dma((2,)),
        ],
        compiler_params=pltpu.CompilerParams(
            collective_id=0, has_side_effects=True, vmem_limit_bytes=56 * 2**20
        ),
    )(clip_lengths, slab_bounds, latents, weights, norm_gain.reshape(1, OWN), norm_bias.reshape(1, OWN))


def solution(mesh):
    placed = (P("chan", "tm", None), P(None, None, None, "chan"), P("chan"), P("chan"), P(), P("tm", None))
    return jax.shard_map(
        shards, mesh=mesh, in_specs=placed, out_specs=P("chan", "tm", None), check_vma=False
    )
```

```python
import jax
import jax.numpy as jnp
from jax import lax
from jax.experimental import pallas as pl
from jax.experimental.pallas import tpu as pltpu
from jax.sharding import PartitionSpec as P

MESH = pl.DeviceIdType.MESH
F32 = jnp.float32
BF16 = jnp.bfloat16

GROUPS = 32
NCLIP = 12
SLABS = 64
RING = 4
MOST = 6
FRAMES = 4
CAP = 8
CELLS = 512
ROW = 32
OWN = 128
PAIR = 256
HALF = 64
PIECES = 4
WIDTH = 512 // GROUPS
norm_eps = 1e-06


def conv_part(w_ref, side, frames, before_row=lambda a: None):
    lane = lax.broadcasted_iota(jnp.int32, (1, CELLS), 1)
    column = lax.rem(lane, ROW)
    total = None
    for a in range(3):
        before_row(a)
        rows = None
        for b in range(3):
            part = None
            for k in range(3):
                tap = 3 * a + b
                weights = jnp.concatenate([w_ref[side, k, tap, 0], w_ref[side, k, tap, 1]], axis=1)
                term = jnp.dot(weights, frames[k], preferred_element_type=F32)
                part = term if part is None else part + term
            if b == 0:
                part = jnp.where(column > 0, pltpu.roll(part, 1, axis=1), 0.0)
            if b == 2:
                part = jnp.where(column < ROW - 1, pltpu.roll(part, CELLS - 1, axis=1), 0.0)
            rows = part if rows is None else rows + part
        if a == 0:
            rows = jnp.where(lane >= ROW, pltpu.roll(rows, ROW, axis=1), 0.0)
        if a == 2:
            rows = jnp.where(lane < CELLS - ROW, pltpu.roll(rows, CELLS - ROW, axis=1), 0.0)
        total = rows if total is None else total + rows
    return total


def norm_block(summed, residual, gain, bias):
    grouped = summed.reshape(OWN // WIDTH, WIDTH, CELLS)
    scale = 1.0 / (WIDTH * CELLS)
    average = jnp.sum(jnp.sum(grouped, axis=1, keepdims=True), axis=2, keepdims=True) * scale
    centred = grouped - average
    variance = jnp.sum(jnp.sum(centred * centred, axis=1, keepdims=True), axis=2, keepdims=True) * scale
    normed = (centred * lax.rsqrt(variance + norm_eps)).reshape(OWN, CELLS) * gain + bias
    return (normed / (1.0 + jnp.exp(-normed)) + residual.astype(F32)).astype(BF16)


def coded(summed):
    grouped = summed.reshape(OWN // WIDTH, WIDTH, CELLS)
    top = jnp.max(jnp.max(jnp.abs(grouped), axis=1, keepdims=True), axis=2, keepdims=True)
    step = jnp.maximum(top, 1e-30) * (1.0 / 32767.0)
    levels = jnp.round(grouped * (1.0 / step)).reshape(OWN, CELLS)
    return levels.astype(jnp.int32).astype(jnp.int16), jnp.broadcast_to(step.reshape(OWN // WIDTH, 1), (OWN // WIDTH, OWN))


def decoded(levels, steps):
    grouped = levels.astype(jnp.int32).astype(F32).reshape(OWN // WIDTH, WIDTH, CELLS)
    return (grouped * steps[:, 0:1].reshape(OWN // WIDTH, 1, 1)).reshape(OWN, CELLS)


def kernel(
    clips, bounds, x_hbm, w_ref, gain_ref, bias_ref, out_ref,
    x_ref, slots, xn, weights, acc, q_out, q_in, step_out, step_in, blocks, column_pair, relay, relay_blk,
    local_sem, sib_s, sib_r, halo_s, halo_r, hfwd_s, hfwd_r, q_s, q_r, step_s, step_r, blk_s, blk_r, relay_s, relay_r, edge_s, edge_r, half_s, half_r, on_s, on_r, ext_s, ext_r, efwd_s, efwd_r,
):
    t, c = lax.axis_index("tm"), lax.axis_index("chan")
    p, core = lax.div(c, 2), lax.rem(c, 2)
    core_else = 1 - core
    c_sib, c_far, c_cross = 2 * p + core_else, 2 * (1 - p) + core, 2 * (1 - p) + core_else
    t_next, t_prev = lax.rem(t + 1, SLABS), lax.rem(t + SLABS - 1, SLABS)
    has_next, has_prev = t < SLABS - 1, t > 0
    x = lax.rem(t, RING)
    at_low, at_high = x == 0, x == RING - 1
    not_low, not_high = x > 0, x < RING - 1
    ring_next, ring_prev = t < SLABS - RING, t >= RING

    def slab(step):
        return lax.rem(t + SLABS + step, SLABS)

    extra = at_high & has_next
    mine = pl.ds(pl.multiple_of(core * OWN, OWN), OWN)
    theirs = pl.ds(pl.multiple_of(core_else * OWN, OWN), OWN)

    barrier = pltpu.get_barrier_semaphore()

    def greet(partner):
        pl.semaphore_signal(barrier, inc=1, device_id=partner, device_id_type=MESH)

    partners = [(has_next, 1), (has_prev, -1), (at_high, -2), (at_high, -3)]
    partners += [((x == 2) & ring_next, 2), (x == 1, 2), ((x == 1) & ring_next, 3)]
    partners += [(at_low, 3), (at_low & ring_next, 4)] + [(at_low & ring_prev, -step) for step in (2, 3, 4)]
    greet((t, c_sib))
    greet((t, c_far))
    for when, step in partners:
        pl.when(when)(lambda step=step: greet((slab(step), c)))

    def outputs_of(member):
        return pl.ds(pl.multiple_of(member * OWN, OWN), OWN)

    own_x = pltpu.make_async_copy(x_hbm, x_ref, local_sem.at[2])
    own_x.start()
    own_w = [
        pltpu.make_async_copy(w_ref.at[:, :, outputs_of(member), :], weights.at[side, :, :, core], local_sem.at[side])
        for side, member in enumerate((c_far, c))
    ]
    for copy in own_w:
        copy.start()
    column_pair[0] = jnp.transpose(jnp.broadcast_to(gain_ref[...], (OWN, OWN)))
    column_pair[1] = jnp.transpose(jnp.broadcast_to(bias_ref[...], (OWN, OWN)))
    own_x.wait()
    for f in (3, 2, 1):
        xn[2 + f, mine, :] = x_ref[:, f, :]
    pl.semaphore_wait(barrier, 2 + sum(when.astype(jnp.int32) for when, _ in partners))

    def send(src, dst, s, r, device):
        return pltpu.make_async_remote_copy(
            src_ref=src, dst_ref=dst, send_sem=s, recv_sem=r, device_id=device, device_id_type=MESH
        )

    started = []

    def go(copy, when=None, keep=True):
        if when is None:
            copy.start()
        else:
            pl.when(when)(copy.start)
        if keep:
            started.append((copy, when))

    def share_x(f):
        go(send(xn.at[2 + f, mine], xn.at[2 + f, mine], sib_s.at[f], sib_r.at[f], (t, c_sib)))

    def share_w(side, rows, n):
        src = w_ref.at[:, rows, outputs_of((c_cross, c_sib)[side]), :]
        go(send(src, weights.at[side, :, rows, core], sib_s.at[n], sib_r.at[n], (t, c_sib)))

    for f in (3, 2, 1):
        share_x(f)
    for a in range(3):
        share_w(0, pl.ds(3 * a, 3), 4 + a)
    xn[2, mine, :] = x_ref[:, 0, :]
    share_x(0)
    go(send(xn.at[5, mine], xn.at[1, mine], halo_s.at[1], halo_r.at[1], (t_next, c)), has_next)
    go(send(xn.at[4, mine], xn.at[0, mine], halo_s.at[0], halo_r.at[0], (t_next, c)), has_next & not_high)
    halves = [pl.ds(pl.multiple_of(core * OWN + HALF * part, HALF), HALF) for part in range(2)]
    for part in range(2):
        go(send(xn.at[4, halves[part]], relay.at[part], edge_s.at[part], relay_r.at[part], (slab(-3), c)), has_next & at_high)
    for h in range(2):
        go(send(xn.at[2 + h, mine], xn.at[6 + h, mine], ext_s.at[h], ext_r.at[h], (t_prev, c)), has_prev & at_low)

    share_w(1, pl.ds(0, 9), 7)

    def arrived(dst, r, when=None):
        copy = pltpu.make_async_remote_copy(
            src_ref=dst, dst_ref=dst, send_sem=r, recv_sem=r, device_id=(t, c), device_id_type=MESH
        )
        if when is None:
            copy.wait_recv()
        else:
            pl.when(when)(copy.wait_recv)

    passed = [send(xn.at[h, mine], xn.at[h, mine], hfwd_s.at[h], hfwd_r.at[h], (t, c_sib)) for h in range(2)]
    started += [(copy, has_prev) for copy in passed]

    def pass_halo(h, relayed=False):
        if relayed:
            for part in range(2):
                arrived(xn.at[h, halves[part]], edge_r.at[part])
        else:
            arrived(xn.at[h, mine], halo_r.at[h])
        passed[h].start()

    def await_halo(h):
        arrived(xn.at[h, theirs], hfwd_r.at[h])

    def relay_halo():
        for part in range(2):
            arrived(relay.at[part], relay_r.at[part], at_low & ring_next)
            dst = xn.at[0, halves[part]]
            go(send(relay.at[part], dst, relay_s.at[part], edge_r.at[part], (slab(4), c)), at_low & ring_next)

    def relay_block(f, part):
        n, when = 2 * (3 - f) + part, (x == 2 - part) & ring_next
        arrived(relay_blk.at[n], half_r.at[n], when)
        dst = blocks.at[f - 2, pl.ds(HALF * part, HALF)]
        go(send(relay_blk.at[n], dst, on_s.at[n], on_r.at[n], (slab(2 + part), c)), when)

    extra_passed = [send(xn.at[6 + h, mine], xn.at[6 + h, mine], efwd_s.at[h], efwd_r.at[h], (t, c_sib)) for h in range(2)]
    started += [(copy, extra) for copy in extra_passed]

    def pass_extra(h):
        arrived(xn.at[6 + h, mine], ext_r.at[h])
        extra_passed[h].start()

    def await_extra(h):
        arrived(xn.at[6 + h, theirs], efwd_r.at[h])

    def sources(f):
        frame = t * FRAMES + f
        first, end = jnp.int32(0), jnp.int32(0)
        for n in range(NCLIP):
            first = jnp.where(end <= frame, end, first)
            end = end + clips[n]
        own = xn[f + 2]
        before = jnp.where(first <= frame - 1, xn[f + 1], own)
        earlier = jnp.where(first <= frame - 2, xn[f], before)
        return earlier, before, own

    def theirs_of(f, keep=True, before_row=lambda a: None):
        levels, steps = coded(conv_part(weights, 0, sources(f), before_row))
        q_out[f] = levels
        step_out[f] = steps
        go(send(q_out.at[f], q_in.at[f], q_s.at[f], q_r.at[f], (t, c_far)), None, keep)
        go(send(step_out.at[f], step_in.at[f], step_s.at[f], step_r.at[f], (t, c_far)), None, keep)

    def own_of(f):
        acc[f] = conv_part(weights, 1, sources(f))

    def merge(f):
        arrived(q_in.at[f], q_r.at[f])
        arrived(step_in.at[f], step_r.at[f])
        summed = acc[f] + decoded(q_in[f], step_in[f])
        gain, bias = column_pair[0, :, 0:1], column_pair[1, :, 0:1]
        blocks[2 + f] = norm_block(summed, xn[2 + f, mine, :], gain, bias)

    def finish(f):
        merge(f)
        if f < 2:
            go(send(blocks.at[2 + f], blocks.at[6 + f], blk_s.at[f], blk_r.at[f], (t_prev, c)), has_prev & not_low)
            return
        go(send(blocks.at[2 + f], blocks.at[f - 2], blk_s.at[f], blk_r.at[f], (t_next, c)), has_next & not_high)
        for part in range(2):
            n = 2 * (3 - f) + part
            src = blocks.at[2 + f, pl.ds(HALF * part, HALF)]
            go(send(src, relay_blk.at[n], half_s.at[n], half_r.at[n], (slab(-1 - part), c)), has_next & at_high)

    @pl.when(jnp.logical_not(has_prev))
    def _():
        for h in range(2):
            xn[h] = jnp.zeros((PAIR, CELLS), BF16)
            blocks[h] = jnp.zeros((OWN, CELLS), BF16)

    @pl.when(jnp.logical_not(has_next))
    def _():
        for h in range(2):
            blocks[6 + h] = jnp.zeros((OWN, CELLS), BF16)

    def await_row(a):
        rows = pl.ds(3 * a, 3)
        arrived(weights.at[0, :, rows, core_else], sib_r.at[4 + a])

    own_w[0].wait()
    for f in (3, 2, 1):
        arrived(xn.at[2 + f, theirs], sib_r.at[f])
    theirs_of(3, before_row=await_row)
    arrived(xn.at[2, theirs], sib_r.at[0])
    theirs_of(2)
    pl.when(not_low)(lambda: pass_halo(1))
    own_w[1].wait()
    arrived(weights.at[1, :, :, core_else], sib_r.at[7])
    own_of(3)
    relay_halo()

    @pl.when(not_low)
    def _():
        await_halo(1)
        theirs_of(1, False)
        pass_halo(0)

    own_of(2)
    finish(3)
    pl.when(extra)(lambda: pass_extra(0))

    @pl.when(not_low)
    def _():
        await_halo(0)
        theirs_of(0, False)

    @pl.when(at_low)
    def _():
        pl.when(has_prev)(lambda: (pass_halo(1), await_halo(1))[0])
        theirs_of(1, False)

    own_of(1)
    finish(2)
    pl.when(at_low & has_prev)(lambda: (pass_halo(0, True), await_halo(0))[0])
    pl.when(at_low)(lambda: theirs_of(0, False))
    own_of(0)

    @pl.when(extra)
    def _():
        await_extra(0)
        theirs_of(4, False)
        pass_extra(1)

    relay_block(3, 0)
    finish(1)
    relay_block(3, 1)
    relay_block(2, 0)

    @pl.when(extra)
    def _():
        await_extra(1)
        theirs_of(5, False)

    finish(0)
    relay_block(2, 1)

    @pl.when(extra)
    def _():
        def both(f, carry):
            own_of(f)
            merge(f)
            return carry

        lax.fori_loop(FRAMES, FRAMES + 2, both, 0)

    for f in range(FRAMES):
        slot, when = (6 + f, has_next & not_high) if f < 2 else (f - 2, not_low)
        arrived(blocks.at[slot], blk_r.at[f], when)
    for f in (3, 2):
        for part in range(2):
            n = 2 * (3 - f) + part
            arrived(blocks.at[f - 2, pl.ds(HALF * part, HALF)], on_r.at[n], at_low & has_prev)

    first, size = bounds[0, 0], bounds[0, 1] - bounds[0, 0]
    offset = first - (t * FRAMES - 2)
    for j in range(CAP):
        value = blocks[jnp.clip(offset + j, 0, CAP - 1)]
        slots[:, j, :] = jnp.where(j < size, value, jnp.zeros_like(value)).astype(F32)
    out_ref[...] = slots[...].astype(BF16)
    for f, when in ((0, None), (1, None), (4, extra), (5, extra)):
        started.append((send(q_out.at[f], q_in.at[f], q_s.at[f], q_r.at[f], (t, c_far)), when))
        started.append((send(step_out.at[f], step_in.at[f], step_s.at[f], step_r.at[f], (t, c_far)), when))
    for copy, when in started:
        if when is None:
            copy.wait_send()
        else:
            pl.when(when)(copy.wait_send)


def hand_over(held, out_ref, space, in_sems, out_sems):
    rows = [pl.ds(n * (OWN // PIECES), OWN // PIECES) for n in range(PIECES)]
    loads = [pltpu.make_async_copy(held.at[r], space.at[r], in_sems.at[n]) for n, r in enumerate(rows)]
    stores = [pltpu.make_async_copy(space.at[r], out_ref.at[r], out_sems.at[n]) for n, r in enumerate(rows)]
    for load in loads:
        load.start()
    for load, store in zip(loads, stores):
        load.wait()
        store.start()
    for store in stores:
        store.wait()


def shards(latents, conv_weight, norm_gain, norm_bias, clip_lengths, slab_bounds):
    weights = jnp.transpose(conv_weight, (1, 2, 0, 3))
    vmem, smem, dma = pltpu.VMEM, pltpu.SMEM, pltpu.SemaphoreType.DMA
    held = pl.pallas_call(
        kernel,
        out_shape=jax.ShapeDtypeStruct((OWN, CAP, CELLS), BF16),
        in_specs=[
            pl.BlockSpec(memory_space=smem),
            pl.BlockSpec(memory_space=smem),
            pl.BlockSpec(memory_space=pl.ANY),
            pl.BlockSpec(memory_space=pl.ANY),
            pl.BlockSpec(memory_space=vmem),
            pl.BlockSpec(memory_space=vmem),
        ],
        out_specs=pl.BlockSpec(memory_space=vmem),
        scratch_shapes=[
            vmem((OWN, FRAMES, CELLS), BF16),
            vmem((OWN, CAP, CELLS), F32),
            vmem((CAP, PAIR, CELLS), BF16),
            vmem((2, 3, 9, 2, OWN, OWN), BF16),
            vmem((MOST, OWN, CELLS), F32),
            vmem((MOST, OWN, CELLS), jnp.int16),
            vmem((MOST, OWN, CELLS), jnp.int16),
            vmem((MOST, OWN // WIDTH, OWN), F32),
            vmem((MOST, OWN // WIDTH, OWN), F32),
            vmem((CAP, OWN, CELLS), BF16),
            vmem((2, OWN, OWN), F32),
            vmem((2, HALF, CELLS), BF16),
            vmem((4, HALF, CELLS), BF16),
            dma((3,)),
            dma((8,)), dma((8,)),
            dma((2,)), dma((2,)),
            dma((2,)), dma((2,)),
            dma((MOST,)), dma((MOST,)),
            dma((MOST,)), dma((MOST,)),
            dma((4,)), dma((4,)),
            dma((2,)), dma((2,)),
            dma((2,)), dma((2,)),
            dma((4,)), dma((4,)),
            dma((4,)), dma((4,)),
            dma((2,)), dma((2,)),
            dma((2,)), dma((2,)),
        ],
        compiler_params=pltpu.CompilerParams(
            collective_id=0, has_side_effects=True, vmem_limit_bytes=56 * 2**20
        ),
    )(clip_lengths, slab_bounds, latents, weights, norm_gain.reshape(1, OWN), norm_bias.reshape(1, OWN))
    return pl.pallas_call(
        hand_over,
        out_shape=jax.ShapeDtypeStruct(held.shape, held.dtype),
        in_specs=[pl.BlockSpec(memory_space=pl.ANY)],
        out_specs=pl.BlockSpec(memory_space=pl.ANY),
        scratch_shapes=[vmem((OWN, CAP, CELLS), BF16), dma((PIECES,)), dma((PIECES,))],
        compiler_params=pltpu.CompilerParams(vmem_limit_bytes=56 * 2**20),
    )(held)


def solution(mesh):
    placed = (P("chan", "tm", None), P(None, None, None, "chan"), P("chan"), P("chan"), P(), P("tm", None))
    return jax.shard_map(
        shards, mesh=mesh, in_specs=placed, out_specs=P("chan", "tm", None), check_vma=False
    )
```

```python
import jax
import jax.numpy as jnp
from jax import lax
from jax.experimental import pallas as pl
from jax.experimental.pallas import tpu as pltpu
from jax.sharding import PartitionSpec as P

MESH = pl.DeviceIdType.MESH
F32 = jnp.float32
BF16 = jnp.bfloat16

GROUPS = 32
NCLIP = 12
SLABS = 64
RING = 4
MOST = 6
FRAMES = 4
CAP = 8
CELLS = 512
ROW = 32
OWN = 128
PAIR = 256
HALF = 64
WIDTH = 512 // GROUPS
norm_eps = 1e-06


def conv_part(w_ref, side, frames, before_row=lambda a: None):
    lane = lax.broadcasted_iota(jnp.int32, (1, CELLS), 1)
    column = lax.rem(lane, ROW)
    total = None
    for a in range(3):
        before_row(a)
        rows = None
        for b in range(3):
            part = None
            for k in range(3):
                tap = 3 * a + b
                weights = jnp.concatenate([w_ref[side, k, tap, 0], w_ref[side, k, tap, 1]], axis=1)
                term = jnp.dot(weights, frames[k], preferred_element_type=F32)
                part = term if part is None else part + term
            if b == 0:
                part = jnp.where(column > 0, pltpu.roll(part, 1, axis=1), 0.0)
            if b == 2:
                part = jnp.where(column < ROW - 1, pltpu.roll(part, CELLS - 1, axis=1), 0.0)
            rows = part if rows is None else rows + part
        if a == 0:
            rows = jnp.where(lane >= ROW, pltpu.roll(rows, ROW, axis=1), 0.0)
        if a == 2:
            rows = jnp.where(lane < CELLS - ROW, pltpu.roll(rows, CELLS - ROW, axis=1), 0.0)
        total = rows if total is None else total + rows
    return total


def norm_block(summed, residual, gain, bias):
    grouped = summed.reshape(OWN // WIDTH, WIDTH, CELLS)
    scale = 1.0 / (WIDTH * CELLS)
    average = jnp.sum(jnp.sum(grouped, axis=1, keepdims=True), axis=2, keepdims=True) * scale
    centred = grouped - average
    variance = jnp.sum(jnp.sum(centred * centred, axis=1, keepdims=True), axis=2, keepdims=True) * scale
    normed = (centred * lax.rsqrt(variance + norm_eps)).reshape(OWN, CELLS) * gain + bias
    return (normed / (1.0 + jnp.exp(-normed)) + residual.astype(F32)).astype(BF16)


def coded(summed):
    grouped = summed.reshape(OWN // WIDTH, WIDTH, CELLS)
    top = jnp.max(jnp.max(jnp.abs(grouped), axis=1, keepdims=True), axis=2, keepdims=True)
    step = jnp.maximum(top, 1e-30) * (1.0 / 32767.0)
    levels = jnp.round(grouped * (1.0 / step)).reshape(OWN, CELLS)
    return levels.astype(jnp.int32).astype(jnp.int16), jnp.broadcast_to(step.reshape(OWN // WIDTH, 1), (OWN // WIDTH, OWN))


def decoded(levels, steps):
    grouped = levels.astype(jnp.int32).astype(F32).reshape(OWN // WIDTH, WIDTH, CELLS)
    return (grouped * steps[:, 0:1].reshape(OWN // WIDTH, 1, 1)).reshape(OWN, CELLS)


def kernel(
    clips, bounds, x_hbm, w_ref, gain_ref, bias_ref, out_ref,
    x_ref, slots, xn, weights, acc, q_out, q_in, step_out, step_in, blocks, column_pair, relay, relay_blk,
    local_sem, sib_s, sib_r, halo_s, halo_r, hfwd_s, hfwd_r, q_s, q_r, step_s, step_r, blk_s, blk_r, relay_s, relay_r, edge_s, edge_r, half_s, half_r, on_s, on_r, ext_s, ext_r, efwd_s, efwd_r,
):
    t, c = lax.axis_index("tm"), lax.axis_index("chan")
    p, core = lax.div(c, 2), lax.rem(c, 2)
    core_else = 1 - core
    c_sib, c_far, c_cross = 2 * p + core_else, 2 * (1 - p) + core, 2 * (1 - p) + core_else
    t_next, t_prev = lax.rem(t + 1, SLABS), lax.rem(t + SLABS - 1, SLABS)
    has_next, has_prev = t < SLABS - 1, t > 0
    x = lax.rem(t, RING)
    at_low, at_high = x == 0, x == RING - 1
    not_low, not_high = x > 0, x < RING - 1
    ring_next, ring_prev = t < SLABS - RING, t >= RING

    def slab(step):
        return lax.rem(t + SLABS + step, SLABS)

    extra = at_high & has_next
    mine = pl.ds(pl.multiple_of(core * OWN, OWN), OWN)
    theirs = pl.ds(pl.multiple_of(core_else * OWN, OWN), OWN)

    barrier = pltpu.get_barrier_semaphore()

    def greet(partner):
        pl.semaphore_signal(barrier, inc=1, device_id=partner, device_id_type=MESH)

    partners = [(has_next, 1), (has_prev, -1), (at_high, -2), (at_high, -3)]
    partners += [((x == 2) & ring_next, 2), (x == 1, 2), ((x == 1) & ring_next, 3)]
    partners += [(at_low, 3), (at_low & ring_next, 4)] + [(at_low & ring_prev, -step) for step in (2, 3, 4)]
    greet((t, c_sib))
    greet((t, c_far))
    for when, step in partners:
        pl.when(when)(lambda step=step: greet((slab(step), c)))

    def outputs_of(member):
        return pl.ds(pl.multiple_of(member * OWN, OWN), OWN)

    own_x = pltpu.make_async_copy(x_hbm, x_ref, local_sem.at[2])
    own_x.start()
    own_w = [
        pltpu.make_async_copy(w_ref.at[:, :, outputs_of(member), :], weights.at[side, :, :, core], local_sem.at[side])
        for side, member in enumerate((c_far, c))
    ]
    for copy in own_w:
        copy.start()
    column_pair[0] = jnp.transpose(jnp.broadcast_to(gain_ref[...], (OWN, OWN)))
    column_pair[1] = jnp.transpose(jnp.broadcast_to(bias_ref[...], (OWN, OWN)))
    own_x.wait()
    for f in (3, 2, 1):
        xn[2 + f, mine, :] = x_ref[:, f, :]
    pl.semaphore_wait(barrier, 2 + sum(when.astype(jnp.int32) for when, _ in partners))

    def send(src, dst, s, r, device):
        return pltpu.make_async_remote_copy(
            src_ref=src, dst_ref=dst, send_sem=s, recv_sem=r, device_id=device, device_id_type=MESH
        )

    started = []

    def go(copy, when=None, keep=True):
        if when is None:
            copy.start()
        else:
            pl.when(when)(copy.start)
        if keep:
            started.append((copy, when))

    def share_x(f):
        go(send(xn.at[2 + f, mine], xn.at[2 + f, mine], sib_s.at[f], sib_r.at[f], (t, c_sib)))

    def share_w(side, rows, n):
        src = w_ref.at[:, rows, outputs_of((c_cross, c_sib)[side]), :]
        go(send(src, weights.at[side, :, rows, core], sib_s.at[n], sib_r.at[n], (t, c_sib)))

    for f in (3, 2, 1):
        share_x(f)
    for a in range(3):
        share_w(0, pl.ds(3 * a, 3), 4 + a)
    xn[2, mine, :] = x_ref[:, 0, :]
    share_x(0)
    go(send(xn.at[5, mine], xn.at[1, mine], halo_s.at[1], halo_r.at[1], (t_next, c)), has_next)
    go(send(xn.at[4, mine], xn.at[0, mine], halo_s.at[0], halo_r.at[0], (t_next, c)), has_next & not_high)
    halves = [pl.ds(pl.multiple_of(core * OWN + HALF * part, HALF), HALF) for part in range(2)]
    for part in range(2):
        go(send(xn.at[4, halves[part]], relay.at[part], edge_s.at[part], relay_r.at[part], (slab(-3), c)), has_next & at_high)
    for h in range(2):
        go(send(xn.at[2 + h, mine], xn.at[6 + h, mine], ext_s.at[h], ext_r.at[h], (t_prev, c)), has_prev & at_low)

    share_w(1, pl.ds(0, 9), 7)

    def arrived(dst, r, when=None):
        copy = pltpu.make_async_remote_copy(
            src_ref=dst, dst_ref=dst, send_sem=r, recv_sem=r, device_id=(t, c), device_id_type=MESH
        )
        if when is None:
            copy.wait_recv()
        else:
            pl.when(when)(copy.wait_recv)

    passed = [send(xn.at[h, mine], xn.at[h, mine], hfwd_s.at[h], hfwd_r.at[h], (t, c_sib)) for h in range(2)]
    started += [(copy, has_prev) for copy in passed]

    def pass_halo(h, relayed=False):
        if relayed:
            for part in range(2):
                arrived(xn.at[h, halves[part]], edge_r.at[part])
        else:
            arrived(xn.at[h, mine], halo_r.at[h])
        passed[h].start()

    def await_halo(h):
        arrived(xn.at[h, theirs], hfwd_r.at[h])

    def relay_halo():
        for part in range(2):
            arrived(relay.at[part], relay_r.at[part], at_low & ring_next)
            dst = xn.at[0, halves[part]]
            go(send(relay.at[part], dst, relay_s.at[part], edge_r.at[part], (slab(4), c)), at_low & ring_next)

    def relay_block(f, part):
        n, when = 2 * (3 - f) + part, (x == 2 - part) & ring_next
        arrived(relay_blk.at[n], half_r.at[n], when)
        dst = blocks.at[f - 2, pl.ds(HALF * part, HALF)]
        go(send(relay_blk.at[n], dst, on_s.at[n], on_r.at[n], (slab(2 + part), c)), when)

    extra_passed = [send(xn.at[6 + h, mine], xn.at[6 + h, mine], efwd_s.at[h], efwd_r.at[h], (t, c_sib)) for h in range(2)]
    started += [(copy, extra) for copy in extra_passed]

    def pass_extra(h):
        arrived(xn.at[6 + h, mine], ext_r.at[h])
        extra_passed[h].start()

    def await_extra(h):
        arrived(xn.at[6 + h, theirs], efwd_r.at[h])

    def sources(f):
        frame = t * FRAMES + f
        first, end = jnp.int32(0), jnp.int32(0)
        for n in range(NCLIP):
            first = jnp.where(end <= frame, end, first)
            end = end + clips[n]
        own = xn[f + 2]
        before = jnp.where(first <= frame - 1, xn[f + 1], own)
        earlier = jnp.where(first <= frame - 2, xn[f], before)
        return earlier, before, own

    def theirs_of(f, keep=True, before_row=lambda a: None):
        levels, steps = coded(conv_part(weights, 0, sources(f), before_row))
        q_out[f] = levels
        step_out[f] = steps
        go(send(q_out.at[f], q_in.at[f], q_s.at[f], q_r.at[f], (t, c_far)), None, keep)
        go(send(step_out.at[f], step_in.at[f], step_s.at[f], step_r.at[f], (t, c_far)), None, keep)

    def own_of(f):
        acc[f] = conv_part(weights, 1, sources(f))

    def merge(f):
        arrived(q_in.at[f], q_r.at[f])
        arrived(step_in.at[f], step_r.at[f])
        summed = acc[f] + decoded(q_in[f], step_in[f])
        gain, bias = column_pair[0, :, 0:1], column_pair[1, :, 0:1]
        blocks[2 + f] = norm_block(summed, xn[2 + f, mine, :], gain, bias)

    def finish(f):
        merge(f)
        if f < 2:
            go(send(blocks.at[2 + f], blocks.at[6 + f], blk_s.at[f], blk_r.at[f], (t_prev, c)), has_prev & not_low)
            return
        go(send(blocks.at[2 + f], blocks.at[f - 2], blk_s.at[f], blk_r.at[f], (t_next, c)), has_next & not_high)
        for part in range(2):
            n = 2 * (3 - f) + part
            src = blocks.at[2 + f, pl.ds(HALF * part, HALF)]
            go(send(src, relay_blk.at[n], half_s.at[n], half_r.at[n], (slab(-1 - part), c)), has_next & at_high)

    @pl.when(jnp.logical_not(has_prev))
    def _():
        for h in range(2):
            xn[h] = jnp.zeros((PAIR, CELLS), BF16)
            blocks[h] = jnp.zeros((OWN, CELLS), BF16)

    @pl.when(jnp.logical_not(has_next))
    def _():
        for h in range(2):
            blocks[6 + h] = jnp.zeros((OWN, CELLS), BF16)

    def await_row(a):
        rows = pl.ds(3 * a, 3)
        arrived(weights.at[0, :, rows, core_else], sib_r.at[4 + a])

    own_w[0].wait()
    for f in (3, 2, 1):
        arrived(xn.at[2 + f, theirs], sib_r.at[f])
    theirs_of(3, before_row=await_row)
    arrived(xn.at[2, theirs], sib_r.at[0])
    theirs_of(2)
    pl.when(not_low)(lambda: pass_halo(1))
    own_w[1].wait()
    arrived(weights.at[1, :, :, core_else], sib_r.at[7])
    own_of(3)
    relay_halo()

    @pl.when(not_low)
    def _():
        await_halo(1)
        theirs_of(1, False)
        pass_halo(0)

    own_of(2)
    finish(3)
    pl.when(extra)(lambda: pass_extra(0))

    @pl.when(not_low)
    def _():
        await_halo(0)
        theirs_of(0, False)

    @pl.when(at_low)
    def _():
        pl.when(has_prev)(lambda: (pass_halo(1), await_halo(1))[0])
        theirs_of(1, False)

    own_of(1)
    finish(2)
    pl.when(at_low & has_prev)(lambda: (pass_halo(0, True), await_halo(0))[0])
    pl.when(at_low)(lambda: theirs_of(0, False))
    own_of(0)

    @pl.when(extra)
    def _():
        await_extra(0)
        theirs_of(4, False)
        pass_extra(1)

    relay_block(3, 0)
    finish(1)
    relay_block(3, 1)
    relay_block(2, 0)

    @pl.when(extra)
    def _():
        await_extra(1)
        theirs_of(5, False)

    finish(0)
    relay_block(2, 1)

    @pl.when(extra)
    def _():
        def both(f, carry):
            own_of(f)
            merge(f)
            return carry

        lax.fori_loop(FRAMES, FRAMES + 2, both, 0)

    for f in range(FRAMES):
        slot, when = (6 + f, has_next & not_high) if f < 2 else (f - 2, not_low)
        arrived(blocks.at[slot], blk_r.at[f], when)
    for f in (3, 2):
        for part in range(2):
            n = 2 * (3 - f) + part
            arrived(blocks.at[f - 2, pl.ds(HALF * part, HALF)], on_r.at[n], at_low & has_prev)

    first, size = bounds[0, 0], bounds[0, 1] - bounds[0, 0]
    offset = first - (t * FRAMES - 2)
    for j in range(CAP):
        value = blocks[jnp.clip(offset + j, 0, CAP - 1)]
        slots[:, j, :] = jnp.where(j < size, value, jnp.zeros_like(value)).astype(F32)
    out_ref[...] = slots[...].astype(BF16)
    for f, when in ((0, None), (1, None), (4, extra), (5, extra)):
        started.append((send(q_out.at[f], q_in.at[f], q_s.at[f], q_r.at[f], (t, c_far)), when))
        started.append((send(step_out.at[f], step_in.at[f], step_s.at[f], step_r.at[f], (t, c_far)), when))
    for copy, when in started:
        if when is None:
            copy.wait_send()
        else:
            pl.when(when)(copy.wait_send)


def shards(latents, conv_weight, norm_gain, norm_bias, clip_lengths, slab_bounds):
    weights = jnp.transpose(conv_weight, (1, 2, 0, 3))
    vmem, smem, dma = pltpu.VMEM, pltpu.SMEM, pltpu.SemaphoreType.DMA
    return pl.pallas_call(
        kernel,
        out_shape=vmem((OWN, CAP, CELLS), BF16),
        in_specs=[
            pl.BlockSpec(memory_space=smem),
            pl.BlockSpec(memory_space=smem),
            pl.BlockSpec(memory_space=pl.ANY),
            pl.BlockSpec(memory_space=pl.ANY),
            pl.BlockSpec(memory_space=vmem),
            pl.BlockSpec(memory_space=vmem),
        ],
        out_specs=pl.BlockSpec(memory_space=vmem),
        scratch_shapes=[
            vmem((OWN, FRAMES, CELLS), BF16),
            vmem((OWN, CAP, CELLS), F32),
            vmem((CAP, PAIR, CELLS), BF16),
            vmem((2, 3, 9, 2, OWN, OWN), BF16),
            vmem((MOST, OWN, CELLS), F32),
            vmem((MOST, OWN, CELLS), jnp.int16),
            vmem((MOST, OWN, CELLS), jnp.int16),
            vmem((MOST, OWN // WIDTH, OWN), F32),
            vmem((MOST, OWN // WIDTH, OWN), F32),
            vmem((CAP, OWN, CELLS), BF16),
            vmem((2, OWN, OWN), F32),
            vmem((2, HALF, CELLS), BF16),
            vmem((4, HALF, CELLS), BF16),
            dma((3,)),
            dma((8,)), dma((8,)),
            dma((2,)), dma((2,)),
            dma((2,)), dma((2,)),
            dma((MOST,)), dma((MOST,)),
            dma((MOST,)), dma((MOST,)),
            dma((4,)), dma((4,)),
            dma((2,)), dma((2,)),
            dma((2,)), dma((2,)),
            dma((4,)), dma((4,)),
            dma((4,)), dma((4,)),
            dma((2,)), dma((2,)),
            dma((2,)), dma((2,)),
        ],
        compiler_params=pltpu.CompilerParams(
            collective_id=0, has_side_effects=True, vmem_limit_bytes=56 * 2**20
        ),
    )(clip_lengths, slab_bounds, latents, weights, norm_gain.reshape(1, OWN), norm_bias.reshape(1, OWN))


def solution(mesh):
    placed = (P("chan", "tm", None), P(None, None, None, "chan"), P("chan"), P("chan"), P(), P("tm", None))
    return jax.shard_map(
        shards, mesh=mesh, in_specs=placed, out_specs=P("chan", "tm", None), check_vma=False
    )
```

```python
import jax
import jax.numpy as jnp
from jax import lax
from jax.experimental import pallas as pl
from jax.experimental.pallas import tpu as pltpu
from jax.sharding import PartitionSpec as P

MESH = pl.DeviceIdType.MESH
F32 = jnp.float32
BF16 = jnp.bfloat16

GROUPS = 32
NCLIP = 12
SLABS = 64
RING = 4
MOST = 6
FRAMES = 4
CAP = 8
CELLS = 512
ROW = 32
OWN = 128
PAIR = 256
HALF = 64
WIDTH = 512 // GROUPS
norm_eps = 1e-06


def conv_part(w_ref, side, frames, before_row=lambda a: None):
    lane = lax.broadcasted_iota(jnp.int32, (1, CELLS), 1)
    column = lax.rem(lane, ROW)
    total = None
    for a in range(3):
        before_row(a)
        rows = None
        for b in range(3):
            part = None
            for k in range(3):
                tap = 3 * a + b
                weights = jnp.concatenate([w_ref[side, k, tap, 0], w_ref[side, k, tap, 1]], axis=1)
                term = jnp.dot(weights, frames[k], preferred_element_type=F32)
                part = term if part is None else part + term
            if b == 0:
                part = jnp.where(column > 0, pltpu.roll(part, 1, axis=1), 0.0)
            if b == 2:
                part = jnp.where(column < ROW - 1, pltpu.roll(part, CELLS - 1, axis=1), 0.0)
            rows = part if rows is None else rows + part
        if a == 0:
            rows = jnp.where(lane >= ROW, pltpu.roll(rows, ROW, axis=1), 0.0)
        if a == 2:
            rows = jnp.where(lane < CELLS - ROW, pltpu.roll(rows, CELLS - ROW, axis=1), 0.0)
        total = rows if total is None else total + rows
    return total


def norm_block(summed, residual, gain, bias):
    grouped = summed.reshape(OWN // WIDTH, WIDTH, CELLS)
    scale = 1.0 / (WIDTH * CELLS)
    average = jnp.sum(jnp.sum(grouped, axis=1, keepdims=True), axis=2, keepdims=True) * scale
    centred = grouped - average
    variance = jnp.sum(jnp.sum(centred * centred, axis=1, keepdims=True), axis=2, keepdims=True) * scale
    normed = (centred * lax.rsqrt(variance + norm_eps)).reshape(OWN, CELLS) * gain + bias
    return (normed / (1.0 + jnp.exp(-normed)) + residual.astype(F32)).astype(BF16)


def coded(summed):
    grouped = summed.reshape(OWN // WIDTH, WIDTH, CELLS)
    top = jnp.max(jnp.max(jnp.abs(grouped), axis=1, keepdims=True), axis=2, keepdims=True)
    step = jnp.maximum(top, 1e-30) * (1.0 / 32767.0)
    levels = jnp.round(grouped * (1.0 / step)).reshape(OWN, CELLS)
    return levels.astype(jnp.int32).astype(jnp.int16), jnp.broadcast_to(step.reshape(OWN // WIDTH, 1), (OWN // WIDTH, OWN))


def decoded(levels, steps):
    grouped = levels.astype(jnp.int32).astype(F32).reshape(OWN // WIDTH, WIDTH, CELLS)
    return (grouped * steps[:, 0:1].reshape(OWN // WIDTH, 1, 1)).reshape(OWN, CELLS)


def kernel(
    clips, bounds, x_hbm, w_ref, gain_ref, bias_ref, out_ref,
    x_ref, slots, xn, weights, acc, q_out, q_in, step_out, step_in, blocks, column_pair, relay, relay_blk,
    local_sem, sib_s, sib_r, halo_s, halo_r, hfwd_s, hfwd_r, q_s, q_r, step_s, step_r, blk_s, blk_r, relay_s, relay_r, edge_s, edge_r, half_s, half_r, on_s, on_r, ext_s, ext_r, efwd_s, efwd_r,
):
    t, c = lax.axis_index("tm"), lax.axis_index("chan")
    p, core = lax.div(c, 2), lax.rem(c, 2)
    core_else = 1 - core
    c_sib, c_far, c_cross = 2 * p + core_else, 2 * (1 - p) + core, 2 * (1 - p) + core_else
    t_next, t_prev = lax.rem(t + 1, SLABS), lax.rem(t + SLABS - 1, SLABS)
    has_next, has_prev = t < SLABS - 1, t > 0
    x = lax.rem(t, RING)
    at_low, at_high = x == 0, x == RING - 1
    not_low, not_high = x > 0, x < RING - 1
    ring_next, ring_prev = t < SLABS - RING, t >= RING

    def slab(step):
        return lax.rem(t + SLABS + step, SLABS)

    extra = at_high & has_next
    mine = pl.ds(pl.multiple_of(core * OWN, OWN), OWN)
    theirs = pl.ds(pl.multiple_of(core_else * OWN, OWN), OWN)

    barrier = pltpu.get_barrier_semaphore()

    def greet(partner):
        pl.semaphore_signal(barrier, inc=1, device_id=partner, device_id_type=MESH)

    partners = [(has_next, 1), (has_prev, -1), (at_high, -2), (at_high, -3)]
    partners += [((x == 2) & ring_next, 2), (x == 1, 2), ((x == 1) & ring_next, 3)]
    partners += [(at_low, 3), (at_low & ring_next, 4)] + [(at_low & ring_prev, -step) for step in (2, 3, 4)]
    greet((t, c_sib))
    greet((t, c_far))
    for when, step in partners:
        pl.when(when)(lambda step=step: greet((slab(step), c)))

    def outputs_of(member):
        return pl.ds(pl.multiple_of(member * OWN, OWN), OWN)

    own_x = pltpu.make_async_copy(x_hbm, x_ref, local_sem.at[2])
    own_x.start()
    own_w = [
        pltpu.make_async_copy(w_ref.at[:, :, outputs_of(member), :], weights.at[side, :, :, core], local_sem.at[side])
        for side, member in enumerate((c_far, c))
    ]
    for copy in own_w:
        copy.start()
    column_pair[0] = jnp.transpose(jnp.broadcast_to(gain_ref[...], (OWN, OWN)))
    column_pair[1] = jnp.transpose(jnp.broadcast_to(bias_ref[...], (OWN, OWN)))
    own_x.wait()
    for f in (3, 2, 1):
        xn[2 + f, mine, :] = x_ref[:, f, :]
    pl.semaphore_wait(barrier, 2 + sum(when.astype(jnp.int32) for when, _ in partners))

    def send(src, dst, s, r, device):
        return pltpu.make_async_remote_copy(
            src_ref=src, dst_ref=dst, send_sem=s, recv_sem=r, device_id=device, device_id_type=MESH
        )

    started = []

    def go(copy, when=None, keep=True):
        if when is None:
            copy.start()
        else:
            pl.when(when)(copy.start)
        if keep:
            started.append((copy, when))

    def share_x(f):
        go(send(xn.at[2 + f, mine], xn.at[2 + f, mine], sib_s.at[f], sib_r.at[f], (t, c_sib)))

    def share_w(side, rows, n):
        src = w_ref.at[:, rows, outputs_of((c_cross, c_sib)[side]), :]
        go(send(src, weights.at[side, :, rows, core], sib_s.at[n], sib_r.at[n], (t, c_sib)))

    for f in (3, 2, 1):
        share_x(f)
    share_w(0, pl.ds(0, 3), 4)
    go(send(xn.at[5, mine], xn.at[1, mine], halo_s.at[1], halo_r.at[1], (t_next, c)), has_next)
    go(send(xn.at[4, mine], xn.at[0, mine], halo_s.at[0], halo_r.at[0], (t_next, c)), has_next & not_high)
    halves = [pl.ds(pl.multiple_of(core * OWN + HALF * part, HALF), HALF) for part in range(2)]
    for part in range(2):
        go(send(xn.at[4, halves[part]], relay.at[part], edge_s.at[part], relay_r.at[part], (slab(-3), c)), has_next & at_high)
    for a in (1, 2):
        share_w(0, pl.ds(3 * a, 3), 4 + a)
    xn[2, mine, :] = x_ref[:, 0, :]
    share_x(0)
    for h in range(2):
        go(send(xn.at[2 + h, mine], xn.at[6 + h, mine], ext_s.at[h], ext_r.at[h], (t_prev, c)), has_prev & at_low)

    share_w(1, pl.ds(0, 9), 7)

    def arrived(dst, r, when=None):
        copy = pltpu.make_async_remote_copy(
            src_ref=dst, dst_ref=dst, send_sem=r, recv_sem=r, device_id=(t, c), device_id_type=MESH
        )
        if when is None:
            copy.wait_recv()
        else:
            pl.when(when)(copy.wait_recv)

    passed = [send(xn.at[h, mine], xn.at[h, mine], hfwd_s.at[h], hfwd_r.at[h], (t, c_sib)) for h in range(2)]
    started += [(copy, has_prev) for copy in passed]

    def pass_halo(h, relayed=False):
        if relayed:
            for part in range(2):
                arrived(xn.at[h, halves[part]], edge_r.at[part])
        else:
            arrived(xn.at[h, mine], halo_r.at[h])
        passed[h].start()

    def await_halo(h):
        arrived(xn.at[h, theirs], hfwd_r.at[h])

    def relay_halo():
        for part in range(2):
            arrived(relay.at[part], relay_r.at[part], at_low & ring_next)
            dst = xn.at[0, halves[part]]
            go(send(relay.at[part], dst, relay_s.at[part], edge_r.at[part], (slab(4), c)), at_low & ring_next)

    def relay_block(f, part):
        n, when = 2 * (3 - f) + part, (x == 2 - part) & ring_next
        arrived(relay_blk.at[n], half_r.at[n], when)
        dst = blocks.at[f - 2, pl.ds(HALF * part, HALF)]
        go(send(relay_blk.at[n], dst, on_s.at[n], on_r.at[n], (slab(2 + part), c)), when)

    extra_passed = [send(xn.at[6 + h, mine], xn.at[6 + h, mine], efwd_s.at[h], efwd_r.at[h], (t, c_sib)) for h in range(2)]
    started += [(copy, extra) for copy in extra_passed]

    def pass_extra(h):
        arrived(xn.at[6 + h, mine], ext_r.at[h])
        extra_passed[h].start()

    def await_extra(h):
        arrived(xn.at[6 + h, theirs], efwd_r.at[h])

    def sources(f):
        frame = t * FRAMES + f
        first, end = jnp.int32(0), jnp.int32(0)
        for n in range(NCLIP):
            first = jnp.where(end <= frame, end, first)
            end = end + clips[n]
        own = xn[f + 2]
        before = jnp.where(first <= frame - 1, xn[f + 1], own)
        earlier = jnp.where(first <= frame - 2, xn[f], before)
        return earlier, before, own

    def theirs_of(f, keep=True, before_row=lambda a: None):
        levels, steps = coded(conv_part(weights, 0, sources(f), before_row))
        q_out[f] = levels
        step_out[f] = steps
        go(send(q_out.at[f], q_in.at[f], q_s.at[f], q_r.at[f], (t, c_far)), None, keep)
        go(send(step_out.at[f], step_in.at[f], step_s.at[f], step_r.at[f], (t, c_far)), None, keep)

    def own_of(f):
        acc[f] = conv_part(weights, 1, sources(f))

    def merge(f):
        arrived(q_in.at[f], q_r.at[f])
        arrived(step_in.at[f], step_r.at[f])
        summed = acc[f] + decoded(q_in[f], step_in[f])
        gain, bias = column_pair[0, :, 0:1], column_pair[1, :, 0:1]
        blocks[2 + f] = norm_block(summed, xn[2 + f, mine, :], gain, bias)

    def finish(f):
        merge(f)
        if f < 2:
            go(send(blocks.at[2 + f], blocks.at[6 + f], blk_s.at[f], blk_r.at[f], (t_prev, c)), has_prev & not_low)
            return
        go(send(blocks.at[2 + f], blocks.at[f - 2], blk_s.at[f], blk_r.at[f], (t_next, c)), has_next & not_high)
        for part in range(2):
            n = 2 * (3 - f) + part
            src = blocks.at[2 + f, pl.ds(HALF * part, HALF)]
            go(send(src, relay_blk.at[n], half_s.at[n], half_r.at[n], (slab(-1 - part), c)), has_next & at_high)

    @pl.when(jnp.logical_not(has_prev))
    def _():
        for h in range(2):
            xn[h] = jnp.zeros((PAIR, CELLS), BF16)
            blocks[h] = jnp.zeros((OWN, CELLS), BF16)

    @pl.when(jnp.logical_not(has_next))
    def _():
        for h in range(2):
            blocks[6 + h] = jnp.zeros((OWN, CELLS), BF16)

    def await_row(a):
        rows = pl.ds(3 * a, 3)
        arrived(weights.at[0, :, rows, core_else], sib_r.at[4 + a])

    own_w[0].wait()
    for f in (3, 2, 1):
        arrived(xn.at[2 + f, theirs], sib_r.at[f])
    theirs_of(3, before_row=await_row)
    arrived(xn.at[2, theirs], sib_r.at[0])
    theirs_of(2)
    pl.when(not_low)(lambda: pass_halo(1))
    own_w[1].wait()
    arrived(weights.at[1, :, :, core_else], sib_r.at[7])
    own_of(3)
    relay_halo()

    @pl.when(not_low)
    def _():
        await_halo(1)
        theirs_of(1, False)
        pass_halo(0)

    own_of(2)
    finish(3)
    pl.when(extra)(lambda: pass_extra(0))

    @pl.when(not_low)
    def _():
        await_halo(0)
        theirs_of(0, False)

    @pl.when(at_low)
    def _():
        pl.when(has_prev)(lambda: (pass_halo(1), await_halo(1))[0])
        theirs_of(1, False)

    own_of(1)
    finish(2)
    pl.when(at_low & has_prev)(lambda: (pass_halo(0, True), await_halo(0))[0])
    pl.when(at_low)(lambda: theirs_of(0, False))
    own_of(0)

    @pl.when(extra)
    def _():
        await_extra(0)
        theirs_of(4, False)
        pass_extra(1)

    relay_block(3, 0)
    finish(1)
    relay_block(3, 1)
    relay_block(2, 0)

    @pl.when(extra)
    def _():
        await_extra(1)
        theirs_of(5, False)

    finish(0)
    relay_block(2, 1)

    @pl.when(extra)
    def _():
        def both(f, carry):
            own_of(f)
            merge(f)
            return carry

        lax.fori_loop(FRAMES, FRAMES + 2, both, 0)

    for f in range(FRAMES):
        slot, when = (6 + f, has_next & not_high) if f < 2 else (f - 2, not_low)
        arrived(blocks.at[slot], blk_r.at[f], when)
    for f in (3, 2):
        for part in range(2):
            n = 2 * (3 - f) + part
            arrived(blocks.at[f - 2, pl.ds(HALF * part, HALF)], on_r.at[n], at_low & has_prev)

    first, size = bounds[0, 0], bounds[0, 1] - bounds[0, 0]
    offset = first - (t * FRAMES - 2)
    for j in range(CAP):
        value = blocks[jnp.clip(offset + j, 0, CAP - 1)]
        slots[:, j, :] = jnp.where(j < size, value, jnp.zeros_like(value)).astype(F32)
    out_ref[...] = slots[...].astype(BF16)
    for f, when in ((0, None), (1, None), (4, extra), (5, extra)):
        started.append((send(q_out.at[f], q_in.at[f], q_s.at[f], q_r.at[f], (t, c_far)), when))
        started.append((send(step_out.at[f], step_in.at[f], step_s.at[f], step_r.at[f], (t, c_far)), when))
    for copy, when in started:
        if when is None:
            copy.wait_send()
        else:
            pl.when(when)(copy.wait_send)


def shards(latents, conv_weight, norm_gain, norm_bias, clip_lengths, slab_bounds):
    weights = jnp.transpose(conv_weight, (1, 2, 0, 3))
    vmem, smem, dma = pltpu.VMEM, pltpu.SMEM, pltpu.SemaphoreType.DMA
    return pl.pallas_call(
        kernel,
        out_shape=vmem((OWN, CAP, CELLS), BF16),
        in_specs=[
            pl.BlockSpec(memory_space=smem),
            pl.BlockSpec(memory_space=smem),
            pl.BlockSpec(memory_space=pl.ANY),
            pl.BlockSpec(memory_space=pl.ANY),
            pl.BlockSpec(memory_space=vmem),
            pl.BlockSpec(memory_space=vmem),
        ],
        out_specs=pl.BlockSpec(memory_space=vmem),
        scratch_shapes=[
            vmem((OWN, FRAMES, CELLS), BF16),
            vmem((OWN, CAP, CELLS), F32),
            vmem((CAP, PAIR, CELLS), BF16),
            vmem((2, 3, 9, 2, OWN, OWN), BF16),
            vmem((MOST, OWN, CELLS), F32),
            vmem((MOST, OWN, CELLS), jnp.int16),
            vmem((MOST, OWN, CELLS), jnp.int16),
            vmem((MOST, OWN // WIDTH, OWN), F32),
            vmem((MOST, OWN // WIDTH, OWN), F32),
            vmem((CAP, OWN, CELLS), BF16),
            vmem((2, OWN, OWN), F32),
            vmem((2, HALF, CELLS), BF16),
            vmem((4, HALF, CELLS), BF16),
            dma((3,)),
            dma((8,)), dma((8,)),
            dma((2,)), dma((2,)),
            dma((2,)), dma((2,)),
            dma((MOST,)), dma((MOST,)),
            dma((MOST,)), dma((MOST,)),
            dma((4,)), dma((4,)),
            dma((2,)), dma((2,)),
            dma((2,)), dma((2,)),
            dma((4,)), dma((4,)),
            dma((4,)), dma((4,)),
            dma((2,)), dma((2,)),
            dma((2,)), dma((2,)),
        ],
        compiler_params=pltpu.CompilerParams(
            collective_id=0, has_side_effects=True, vmem_limit_bytes=56 * 2**20
        ),
    )(clip_lengths, slab_bounds, latents, weights, norm_gain.reshape(1, OWN), norm_bias.reshape(1, OWN))


def solution(mesh):
    placed = (P("chan", "tm", None), P(None, None, None, "chan"), P("chan"), P("chan"), P(), P("tm", None))
    return jax.shard_map(
        shards, mesh=mesh, in_specs=placed, out_specs=P("chan", "tm", None), check_vma=False
    )
```
